256 devices in a mesh: leaf: 64 (over z, x, core), node: 4 (over y).
Axes of the slice: x: 4, y: 4, z: 8, core: 2. Of those that a mesh axis runs over, the one named last changes fastest.
Arguments:
- leaf_blocks: float32 [131072, 512], P(('leaf', 'node')), as said below
- generators: float32 [3, 131072, 256], P(None, ('leaf', 'node'))
- right_side: float32 [131072, 256], P(('leaf', 'node'))
- tree_order: int32 [256, 512], P(('leaf', 'node')), may hold values from 0 to 511, each once within a row
Outputs:
- solution: float32 [131072, 256], P(('leaf', 'node'))
The draws below stay inside these ranges and needn't reach their ends.
Inputs may be any that keep to these rules, and one draw needn't show every extreme that they name: `leaf_blocks`: each block of 512 rows, read as a square matrix, is symmetric positive definite.
All inputs are finite; a program needn't handle non-finite values.
Results may differ from the reference program's by a relative error of at most 0.0001.
Values sent between devices are 32-bit elements; how exact they have to be, the bound alone decides.
A program may use at most 64 MiB of HBM per device.

```python
import math
import jax
import jax.numpy as jnp
from jax import lax

ROWS_DEV = 512
RANK = 256
NRHS = 256
LEVELS = 3
BLOCKS = 256
ROWS = 131072


def common_profile(key):
    return jax.random.normal(key, (LEVELS, BLOCKS), jnp.float32)


def draw_leaf_blocks(key, part):
    key = jax.random.fold_in(key, 11)
    key_factor, key_diag = jax.random.split(key, 2)
    identity = jnp.eye(ROWS_DEV, dtype=jnp.float32)
    diagonal = jax.random.uniform(key_diag, (BLOCKS, ROWS_DEV), jnp.float32, 0.5, 1.5)

    def one_block(index):
        key_block = jax.random.fold_in(key_factor, index)
        factor = jnp.clip(jax.random.normal(key_block, (ROWS_DEV, ROWS_DEV), jnp.float32), -6.0, 6.0)
        product = jnp.dot(factor, factor.T, precision=lax.Precision.HIGHEST) / ROWS_DEV
        return 0.5 * (product + product.T)
    gram_part = lax.map(one_block, jnp.arange(BLOCKS, dtype=jnp.int32))
    blocks = gram_part + identity[None, :, :] * diagonal[:, :, None]
    return blocks.reshape(BLOCKS * ROWS_DEV, ROWS_DEV).astype(jnp.float32)


def draw_generators(key, part):
    profile = common_profile(key)
    key = jax.random.fold_in(key, 23)
    key_base, key_column, key_node = jax.random.split(key, 3)
    shape = (LEVELS, BLOCKS, ROWS_DEV, RANK)
    base = jnp.clip(jax.random.normal(key_base, shape, jnp.float32), -6.0, 6.0)
    directions = []
    for height in range(LEVELS):
        node_dirs = jax.random.normal(jax.random.fold_in(key_node, height), (2 ** height, RANK), jnp.float32) * (2.0 / math.sqrt(RANK))
        directions.append(jnp.repeat(node_dirs, BLOCKS // 2 ** height, axis=0))
    direction = jnp.stack(directions)
    common = profile[:, :, None, None] * direction[:, :, None, :]
    heights = jnp.arange(LEVELS).astype(jnp.float32)
    level_scale = jnp.sqrt(4.0 * 2.0 ** heights / ROWS)[:, None, None, None]
    column_scale = jnp.exp(jax.random.uniform(key_column, (LEVELS, 1, 1, RANK), jnp.float32, math.log(0.3), 0.0))
    gens = level_scale * column_scale * (base + common)
    return gens.reshape(LEVELS, ROWS, RANK).astype(jnp.float32)


def draw_right_side(key, part):
    profile = common_profile(key)
    key = jax.random.fold_in(key, 37)
    key_noise, key_mix = jax.random.split(key)
    shape = (BLOCKS, ROWS_DEV, NRHS)
    noise = jnp.clip(jax.random.normal(key_noise, shape, jnp.float32), -6.0, 6.0)
    mixing = jax.random.normal(key_mix, (LEVELS, NRHS), jnp.float32) * 0.7
    common = profile[0][:, None] * mixing[0][None, :]
    for height in range(1, LEVELS):
        common = common + profile[height][:, None] * mixing[height][None, :]
    values = noise + common[:, None, :]
    return values.reshape(ROWS, NRHS).astype(jnp.float32)


def setup_inputs(seed: int = 0) -> dict:
    splits = jax.random.split(jax.random.key(seed), 5)
    return {
        "leaf_blocks": draw_leaf_blocks(jax.random.fold_in(splits[4], 71), 0),
        "generators": draw_generators(jax.random.fold_in(splits[4], 71), 0),
        "right_side": draw_right_side(jax.random.fold_in(splits[4], 71), 0),
        "tree_order": jax.vmap(lambda own: jax.random.permutation(own, ROWS_DEV))(jax.random.split(splits[3], BLOCKS)).reshape((BLOCKS, ROWS_DEV)).astype(jnp.int32),
    }


PRECISE = lax.Precision.HIGHEST

def lower_solve(factor, values, transposed):
    return lax.linalg.triangular_solve(factor, values, left_side=True, lower=True, transpose_a=transposed)

def stack_block(gens_block, rhs_block):
    return jnp.concatenate([gens_block[height] for height in range(LEVELS)] + [rhs_block], axis=1)

def block_gram(packed):
    block, gens_block, rhs_block = packed
    leaf_factor = jnp.linalg.cholesky(block)
    solved = lower_solve(leaf_factor, stack_block(gens_block, rhs_block), False)
    width = LEVELS * RANK
    return jnp.einsum('ra,rb->ab', solved[:, :width], solved, precision=PRECISE)

def finish_block(packed):
    block, gens_block, rhs_block, coeff_block = packed
    leaf_factor = jnp.linalg.cholesky(block)
    corrected = rhs_block
    for height in range(LEVELS):
        corrected = corrected - jnp.dot(gens_block[height], coeff_block[height], precision=PRECISE)
    return lower_solve(leaf_factor, lower_solve(leaf_factor, corrected, False), True)

def reference(leaf_blocks, generators, right_side, tree_order):
    blocks = leaf_blocks.reshape(BLOCKS, ROWS_DEV, ROWS_DEV)
    gens_blocks = jnp.transpose(generators.reshape(LEVELS, BLOCKS, ROWS_DEV, RANK), (1, 0, 2, 3))
    rhs_blocks = right_side.reshape(BLOCKS, ROWS_DEV, NRHS)
    ordered = jnp.take_along_axis(rhs_blocks, tree_order[:, :, None], axis=1)
    grams = lax.map(block_gram, (blocks, gens_blocks, ordered))
    current = grams.reshape((2 ** LEVELS, BLOCKS // 2 ** LEVELS) + grams.shape[1:]).sum(1)
    identity = jnp.eye(RANK, dtype=jnp.float32)
    factors = [None] * LEVELS
    top_rows = [None] * LEVELS
    for height in range(LEVELS - 1, -1, -1):
        current = current.reshape((2 ** height, 2) + current.shape[1:]).sum(1)
        offset = height * RANK
        header = current[:, offset:offset + RANK, :]
        factor = jnp.linalg.cholesky(identity[None] + header[:, :, offset:offset + RANK])
        scaled = lower_solve(factor, header, False)
        factors[height] = factor
        top_rows[height] = header
        update = jnp.einsum('nra,nrb->nab', scaled[:, :, :offset], scaled, precision=PRECISE)
        kept = current[:, :offset, :] - update
        current = jnp.concatenate([kept[:, :, :offset], kept[:, :, offset + RANK:]], axis=2)
    coeffs = []
    for height in range(LEVELS):
        offset = height * RANK
        header = top_rows[height]
        target = header[:, :, offset + RANK:]
        for upper in range(height):
            parent = jnp.repeat(coeffs[upper], 2 ** (height - upper), axis=0)
            target = target - jnp.einsum('nrs,nsk->nrk', header[:, :, upper * RANK:(upper + 1) * RANK], parent, precision=PRECISE)
        middle = lower_solve(factors[height], target, False)
        coeffs.append(lower_solve(factors[height], middle, True))
    coeff_blocks = jnp.stack([jnp.repeat(coeffs[height], BLOCKS // 2 ** height, axis=0) for height in range(LEVELS)], axis=1)
    tree_solution = lax.map(finish_block, (blocks, gens_blocks, ordered, coeff_blocks))
    block_index = jnp.arange(BLOCKS, dtype=jnp.int32)[:, None]
    solution = jnp.zeros_like(tree_solution).at[block_index, tree_order].set(tree_solution)
    return solution.reshape(ROWS, NRHS)
```

```python
import functools

import jax
import jax.numpy as jnp
from jax import lax
from jax.experimental import pallas as pl
from jax.experimental.pallas import tpu as pltpu
from jax.sharding import PartitionSpec as P

F32 = jnp.float32
BF16 = jnp.bfloat16
MESH = pl.DeviceIdType.MESH
NN = (((1,), (0,)), ((), ()))
NT = (((1,), (1,)), ((), ()))
TN = (((0,), (0,)), ((), ()))
BASE = 128
VMEM_LIMIT = 50 * 2**20


def split(value):
    high = value.astype(BF16)
    return high, (value - high.astype(F32)).astype(BF16)


def dot3(left, right, dims=NN):
    left_high, left_low = split(left)
    right_high, right_low = split(right)
    one = functools.partial(lax.dot_general, dimension_numbers=dims, preferred_element_type=F32)
    return one(left_high, right_high) + (one(left_high, right_low) + one(left_low, right_high))


def dot6(left, right, dims=NN):
    return lax.dot_general(
        left, right, dims, precision=lax.Precision.HIGHEST, preferred_element_type=F32
    )


def permute(one_hot, value, dims):
    high = value.astype(BF16)
    rest = value - high.astype(F32)
    middle = rest.astype(BF16)
    low = (rest - middle.astype(F32)).astype(BF16)
    one = functools.partial(lax.dot_general, dimension_numbers=dims, preferred_element_type=F32)
    return one(one_hot, high) + (one(one_hot, middle) + one(one_hot, low))


def ldl_factor(p):
    p = [list(row) for row in p]
    n = len(p)
    lower = [[None] * n for _ in range(n)]
    pivots = []
    for k in range(n):
        r = 1.0 / p[k][k]
        pivots.append(r)
        raw = [p[i][k] for i in range(n)] if k == 0 else [p[i][k] if i > k else None for i in range(n)]
        for i in range(k + 1, n):
            for j in range(k + 1, i + 1):
                p[i][j] = p[i][j] - r * (raw[i] * raw[j])
        for i in range(k + 1, n):
            lower[i][k] = raw[i] * r
    return lower, pivots


def ldl_solve(lower, pivots, rows):
    n = len(rows)
    y = list(rows)
    for k in range(n):
        for i in range(k + 1, n):
            y[i] = y[i] - lower[i][k] * y[k]
    z = [y[i] * pivots[i] for i in range(n)]
    for k in range(n - 1, -1, -1):
        for i in range(k):
            z[i] = z[i] - lower[k][i] * z[k]
    return z


def base_inverse(a, columns_ref, rows_ref):
    n = a.shape[0]
    count = n // 8
    lane = lax.broadcasted_iota(jnp.int32, (8, n), 1)
    sub = lax.broadcasted_iota(jnp.int32, (8, n), 0)
    a = [a[8 * v : 8 * v + 8, :] for v in range(count)]
    for kb in range(count):
        k = 8 * kb
        slot = kb % 2
        for j in range(8):
            columns_ref[slot, j] = jnp.broadcast_to(a[kb][:, k + j : k + j + 1], (8, n))
        inside = (lane >= k) & (lane < k + 8)
        rows_ref[slot] = jnp.where(inside, jnp.where(lane == sub + k, 1.0, 0.0), a[kb])
        p = [
            [jnp.broadcast_to(columns_ref[slot, j, i : i + 1, :], (8, n)) for j in range(i + 1)]
            for i in range(8)
        ]
        rows = [jnp.broadcast_to(rows_ref[slot, i : i + 1, :], (8, n)) for i in range(8)]
        q = ldl_solve(*ldl_factor(p), rows)
        own = q[0]
        for j in range(1, 8):
            own = jnp.where(sub == j, q[j], own)
        new = {kb: own}
        for m in range(1, count):
            v = (kb + m) % count
            terms = [jnp.broadcast_to(a[v][:, k + j : k + j + 1], (8, n)) * q[j] for j in range(8)]
            while len(terms) > 1:
                terms = [terms[i] + terms[i + 1] for i in range(0, len(terms), 2)]
            new[v] = jnp.where(inside, 0.0, a[v]) - terms[0]
        a = [new[v] for v in range(count)]
    return jnp.concatenate(a, axis=0)


def invert(a_ref, scratch):
    columns_ref, rows_ref, row_block, column_block = scratch
    n = a_ref.shape[0]
    eye = (
        lax.broadcasted_iota(jnp.int32, (BASE, BASE), 0)
        == lax.broadcasted_iota(jnp.int32, (BASE, BASE), 1)
    ).astype(F32)

    def step(kb, carry):
        own = pl.ds(pl.multiple_of(kb * BASE, BASE), BASE)
        pivot = base_inverse(a_ref[own, own], columns_ref, rows_ref)
        row_block[:, :n] = a_ref[own, :]
        row_block[:, own] = eye
        column_block[:n, :] = a_ref[:, own]
        a_ref[:, own] = jnp.zeros((n, BASE), F32)
        q = dot6(pivot, row_block[:, :n])
        a_ref[...] = a_ref[...] - dot6(column_block[:n, :], q)
        a_ref[own, :] = q
        return carry

    lax.fori_loop(0, n // BASE, step, 0)


def invert_scratch(n):
    return [
        pltpu.VMEM((2, 8, 8, BASE), F32),
        pltpu.VMEM((2, 8, BASE), F32),
        pltpu.VMEM((BASE, n), F32),
        pltpu.VMEM((n, BASE), F32),
    ]


PAIRS = ((2, 2), (1, 2), (0, 2), (2, 3), (1, 1), (0, 1), (1, 3), (0, 0), (0, 3))


def one_hot_of(order_ref):
    n = order_ref.shape[1]
    target = lax.broadcasted_iota(jnp.int32, (n, n), 0)
    return jnp.where(target == order_ref[...], 1.0, 0.0).astype(BF16)


def leaf_kernel(leaf_ref, gens_ref, rhs_ref, order_ref, x_ref, gram_ref, inverse, *scratch):
    inverse[...] = leaf_ref[...]
    invert(inverse, scratch)
    high, low = split(inverse[...])
    one = functools.partial(lax.dot_general, dimension_numbers=NN, preferred_element_type=F32)

    def apply(value):
        value_high, value_low = split(value)
        return one(high, value_high) + (one(high, value_low) + one(low, value_high))

    for level in range(3):
        x_ref[level] = apply(gens_ref[level])
    x_ref[3] = apply(permute(one_hot_of(order_ref), rhs_ref[...], TN))
    for index, (a, b) in enumerate(PAIRS):
        product = dot3(gens_ref[a], x_ref[b], TN)
        for half in range(2):
            gram_ref[index, half] = product[:, half * 128 : half * 128 + 128]


def leaf(leaf_blocks, generators, right_side, order):
    rows, rank = leaf_blocks.shape[0], generators.shape[2]
    return pl.pallas_call(
        leaf_kernel,
        out_shape=(
            jax.ShapeDtypeStruct((4, rows, rank), F32),
            jax.ShapeDtypeStruct((9, 2, rank, 128), F32),
        ),
        scratch_shapes=[pltpu.VMEM((rows, rows), F32)] + invert_scratch(rows),
        compiler_params=pltpu.CompilerParams(vmem_limit_bytes=VMEM_LIMIT),
        name="leaf",
    )(leaf_blocks, generators, right_side, order)


def place():
    leaf_index = lax.axis_index("leaf")
    return leaf_index // 8, (leaf_index // 2) % 4, leaf_index % 2, lax.axis_index("node")


def device(z, x, core, y):
    return ((z * 4 + x) * 2 + core, y)


def owned_rows(half, x, core, y):
    return core * 128 + ((x * 4 + y) if half == 0 else (y * 4 + x)) * 8


def exchange_kernel(reduce, blocks, header, z_bit, *refs):
    if reduce:
        (in_ref, head_ref, rest_ref, total, from_core, from_one, from_two, from_z, one, two) = refs[:10]
        core_sem, one_sem, two_sem, z_sem, first_sem, second_sem, last_sem = refs[10:]
    else:
        in_ref, head_ref, rest_ref, total, from_z = refs[:5]
        z_sem, first_sem, second_sem, last_sem = refs[5:]
    z, x, core, y = place()
    across = device(z, x, 1 - core, y)
    z_partner = device(z ^ (1 << z_bit), x, core, y)

    def along(axis, step):
        if axis == "x":
            return lax.rem(x + step, 4), device(z, lax.rem(x + step, 4), core, y)
        return lax.rem(y + step, 4), device(z, x, core, lax.rem(y + step, 4))

    barrier = pltpu.get_barrier_semaphore()
    partners = [across, z_partner] + [along(axis, step)[1] for axis in "xy" for step in (1, 2, 3)]
    for partner in partners:
        pl.semaphore_signal(barrier, inc=1, device_id=partner, device_id_type=MESH)
    pl.semaphore_wait(barrier, len(partners))

    def send(source, target, sems, to):
        copy = pltpu.make_async_remote_copy(
            src_ref=source, dst_ref=target, send_sem=sems.at[0], recv_sem=sems.at[1],
            device_id=to, device_id_type=MESH,
        )
        copy.start()
        return copy

    first_axis, second_axis = ("x", "y"), ("y", "x")
    mine = {"x": x, "y": y}
    if reduce:
        copy = send(in_ref.at[:, :, pl.ds((1 - core) * 128, 128), :], from_core, core_sem, across)
        copy.wait()
        one[...] = in_ref[:, :, pl.ds(core * 128, 128), :] + from_core[...]
        copies = []
        for step in (1, 2, 3):
            for half in range(2):
                index, to = along(first_axis[half], step)
                copies.append(
                    send(one.at[:, half, pl.ds(index * 32, 32), :], from_one.at[step - 1, half],
                         one_sem.at[step - 1, half], to)
                )
        for copy in copies:
            copy.wait()
        for half in range(2):
            own = one[:, half, pl.ds(mine[first_axis[half]] * 32, 32), :]
            two[:, half] = (own + from_one[0, half]) + (from_one[1, half] + from_one[2, half])
        copies = []
        for step in (1, 2, 3):
            for half in range(2):
                index, to = along(second_axis[half], step)
                copies.append(
                    send(two.at[:, half, pl.ds(index * 8, 8), :], from_two.at[step - 1, half],
                         two_sem.at[step - 1, half], to)
                )
        for copy in copies:
            copy.wait()
        for half in range(2):
            own = two[:, half, pl.ds(mine[second_axis[half]] * 8, 8), :]
            total[:, half] = (own + from_two[0, half]) + (from_two[1, half] + from_two[2, half])
        source = total
    else:
        source = in_ref
    copy = send(source, from_z, z_sem, z_partner)
    copy.wait()
    sums = source[...] + from_z[...]
    if blocks > header:
        rest_ref[...] = sums[header:]
    for half in range(2):
        head_ref[:, half, pl.ds(owned_rows(half, x, core, y), 8), :] = sums[:header, half]
    copies = []
    for step in (1, 2, 3):
        for half in range(2):
            part = head_ref.at[:, half, pl.ds(owned_rows(half, x, core, y), 8), :]
            copies.append(
                send(part, part, first_sem.at[step - 1, half], along(second_axis[half], step)[1])
            )
    for copy in copies:
        copy.wait()
    copies = []
    for step in (1, 2, 3):
        for half in range(2):
            part = head_ref.at[:, half, pl.ds(core * 128 + mine[first_axis[half]] * 32, 32), :]
            copies.append(
                send(part, part, second_sem.at[step - 1, half], along(first_axis[half], step)[1])
            )
    for copy in copies:
        copy.wait()
    part = head_ref.at[:, :, pl.ds(core * 128, 128), :]
    send(part, part, last_sem, across).wait()


def exchange(value, header, z_bit, reduce, collective_id):
    blocks = value.shape[0]
    dma = pltpu.SemaphoreType.DMA
    scratch = []
    if reduce:
        scratch = [
            pltpu.VMEM((blocks, 2, 8, 128), F32),
            pltpu.VMEM((blocks, 2, 128, 128), F32),
            pltpu.VMEM((3, 2, blocks, 32, 128), F32),
            pltpu.VMEM((3, 2, blocks, 8, 128), F32),
            pltpu.VMEM((blocks, 2, 8, 128), F32),
            pltpu.VMEM((blocks, 2, 128, 128), F32),
            pltpu.VMEM((blocks, 2, 32, 128), F32),
            dma((2,)), dma((3, 2, 2)), dma((3, 2, 2)),
        ]
    else:
        scratch = [pltpu.VMEM((8, 128), F32), pltpu.VMEM((blocks, 2, 8, 128), F32)]
    scratch += [dma((2,)), dma((3, 2, 2)), dma((3, 2, 2)), dma((2,))]
    rest = max(blocks - header, 1)
    return pl.pallas_call(
        functools.partial(exchange_kernel, reduce, blocks, header, z_bit),
        out_shape=(
            jax.ShapeDtypeStruct((header, 2, 256, 128), F32),
            jax.ShapeDtypeStruct((rest, 2, 8, 128), F32),
        ),
        in_specs=[pl.BlockSpec(memory_space=pltpu.VMEM)],
        out_specs=(pl.BlockSpec(memory_space=pltpu.VMEM), pl.BlockSpec(memory_space=pltpu.VMEM)),
        scratch_shapes=scratch,
        compiler_params=pltpu.CompilerParams(
            collective_id=collective_id, has_side_effects=True, vmem_limit_bytes=VMEM_LIMIT
        ),
        name="exchange",
    )(value)


def whole(ref, index):
    return jnp.concatenate([ref[index, 0], ref[index, 1]], axis=1)


def plus_identity(value):
    n = value.shape[0]
    eye = lax.broadcasted_iota(jnp.int32, (n, n), 0) == lax.broadcasted_iota(jnp.int32, (n, n), 1)
    return value + jnp.where(eye, 1.0, 0.0)


def level_kernel(level, head_ref, rest_ref, out_ref, scaled_ref, inverse, *scratch):
    z, x, core, y = place()
    inverse[...] = plus_identity(whole(head_ref, 0))
    invert(inverse, scratch)
    for upper in range(level):
        scaled_ref[upper] = dot3(inverse[...], whole(head_ref, level - upper), NT)
    scaled_ref[level] = dot3(inverse[...], whole(head_ref, level + 1))
    index = 0
    for a in range(level - 1, -1, -1):
        for b in list(range(a, -1, -1)) + [level]:
            for half in range(2):
                own = pl.ds(owned_rows(half, x, core, y), 8)
                if b == level or b == a:
                    left, right = a, b
                else:
                    left, right = b, a
                rows = jnp.concatenate(
                    [head_ref[level - left, 0, own, :], head_ref[level - left, 1, own, :]], axis=1
                )
                update = dot3(rows, scaled_ref[right, :, half * 128 : half * 128 + 128])
                out_ref[index, half] = rest_ref[index, half] - update
            index += 1


def tree_level(level, head, rest):
    return pl.pallas_call(
        functools.partial(level_kernel, level),
        out_shape=(
            jax.ShapeDtypeStruct(rest.shape, F32),
            jax.ShapeDtypeStruct((level + 1, 256, 256), F32),
        ),
        scratch_shapes=[pltpu.VMEM((256, 256), F32)] + invert_scratch(256),
        compiler_params=pltpu.CompilerParams(vmem_limit_bytes=VMEM_LIMIT),
        name="level",
    )(head, rest)


def finish_kernel(head_ref, one_ref, two_ref, x_ref, order_ref, out_ref, inverse, *scratch):
    inverse[...] = plus_identity(whole(head_ref, 0))
    invert(inverse, scratch)
    c0 = dot3(inverse[...], whole(head_ref, 1))
    c1 = one_ref[1] - dot3(one_ref[0], c0)
    c2 = two_ref[2] - dot3(two_ref[0], c0) - dot3(two_ref[1], c1)
    x = x_ref[3] - dot3(x_ref[0], c0) - dot3(x_ref[1], c1) - dot3(x_ref[2], c2)
    out_ref[...] = permute(one_hot_of(order_ref), x, NN)


def finish(head, one, two, x, order):
    return pl.pallas_call(
        finish_kernel,
        out_shape=jax.ShapeDtypeStruct(x.shape[1:], F32),
        scratch_shapes=[pltpu.VMEM((256, 256), F32)] + invert_scratch(256),
        compiler_params=pltpu.CompilerParams(vmem_limit_bytes=VMEM_LIMIT),
        name="finish",
    )(head, one, two, x, order)


def per_device(leaf_blocks, generators, right_side, tree_order):
    x, gram = leaf(leaf_blocks, generators, right_side, tree_order)
    head, rest = exchange(gram, 4, 0, True, 0)
    rest, two = tree_level(2, head, rest)
    head, rest = exchange(rest, 3, 1, False, 1)
    rest, one = tree_level(1, head, rest)
    head, _ = exchange(rest, 2, 2, False, 2)
    return finish(head, one, two, x, tree_order)


def solution(mesh):
    return jax.shard_map(
        per_device,
        mesh=mesh,
        in_specs=(
            P(("leaf", "node"), None),
            P(None, ("leaf", "node"), None),
            P(("leaf", "node"), None),
            P(("leaf", "node"), None),
        ),
        out_specs=P(("leaf", "node"), None),
        check_vma=False,
    )
```

```python
import functools

import jax
import jax.numpy as jnp
from jax import lax
from jax.experimental import pallas as pl
from jax.experimental.pallas import tpu as pltpu
from jax.sharding import PartitionSpec as P

F32 = jnp.float32
BF16 = jnp.bfloat16
MESH = pl.DeviceIdType.MESH
NN = (((1,), (0,)), ((), ()))
NT = (((1,), (1,)), ((), ()))
TN = (((0,), (0,)), ((), ()))
BASE = 128
VMEM_LIMIT = 50 * 2**20


def split(value):
    high = value.astype(BF16)
    return high, (value - high.astype(F32)).astype(BF16)


def dot3(left, right, dims=NN):
    left_high, left_low = split(left)
    right_high, right_low = split(right)
    one = functools.partial(lax.dot_general, dimension_numbers=dims, preferred_element_type=F32)
    return one(left_high, right_high) + (one(left_high, right_low) + one(left_low, right_high))


def dot6(left, right, dims=NN):
    return lax.dot_general(
        left, right, dims, precision=lax.Precision.HIGHEST, preferred_element_type=F32
    )


def permute(one_hot, value, dims):
    high = value.astype(BF16)
    rest = value - high.astype(F32)
    middle = rest.astype(BF16)
    low = (rest - middle.astype(F32)).astype(BF16)
    one = functools.partial(lax.dot_general, dimension_numbers=dims, preferred_element_type=F32)
    return one(one_hot, high) + (one(one_hot, middle) + one(one_hot, low))


def ldl_factor(p):
    p = [list(row) for row in p]
    n = len(p)
    lower = [[None] * n for _ in range(n)]
    pivots = []
    for k in range(n):
        r = 1.0 / p[k][k]
        pivots.append(r)
        raw = [p[i][k] for i in range(n)] if k == 0 else [p[i][k] if i > k else None for i in range(n)]
        for i in range(k + 1, n):
            for j in range(k + 1, i + 1):
                p[i][j] = p[i][j] - r * (raw[i] * raw[j])
        for i in range(k + 1, n):
            lower[i][k] = raw[i] * r
    return lower, pivots


def ldl_solve(lower, pivots, rows):
    n = len(rows)
    y = list(rows)
    for k in range(n):
        for i in range(k + 1, n):
            y[i] = y[i] - lower[i][k] * y[k]
    z = [y[i] * pivots[i] for i in range(n)]
    for k in range(n - 1, -1, -1):
        for i in range(k):
            z[i] = z[i] - lower[k][i] * z[k]
    return z


def base_inverse(a, columns_ref, rows_ref):
    n = a.shape[0]
    lane8 = lax.broadcasted_iota(jnp.int32, (8, n), 1)
    sub8 = lax.broadcasted_iota(jnp.int32, (8, n), 0)
    lane = lax.broadcasted_iota(jnp.int32, (n, n), 1)
    for kb in range(n // 8):
        k = 8 * kb
        slot = kb % 2
        own = a[k : k + 8, :]
        for j in range(8):
            columns_ref[slot, j] = jnp.broadcast_to(own[:, k + j : k + j + 1], (8, n))
        inside = (lane8 >= k) & (lane8 < k + 8)
        rows_ref[slot] = jnp.where(inside, jnp.where(lane8 == sub8 + k, 1.0, 0.0), own)
        p = [
            [jnp.broadcast_to(columns_ref[slot, j, i : i + 1, :], (8, n)) for j in range(i + 1)]
            for i in range(8)
        ]
        rows = [jnp.broadcast_to(rows_ref[slot, i : i + 1, :], (8, n)) for i in range(8)]
        q = ldl_solve(*ldl_factor(p), rows)
        own = q[0]
        for j in range(1, 8):
            own = jnp.where(sub8 == j, q[j], own)
        rest = jnp.where((lane >= k) & (lane < k + 8), 0.0, a)
        terms = [
            jnp.broadcast_to(a[:, k + j : k + j + 1], (n, n))
            * jnp.broadcast_to(q[j][0:1, :], (n, n))
            for j in range(8)
        ]
        while len(terms) > 1:
            terms = [terms[i] + terms[i + 1] for i in range(0, len(terms), 2)]
        rest = rest - terms[0]
        parts = [rest[:k]] if k else []
        parts.append(own)
        if k + 8 < n:
            parts.append(rest[k + 8 :])
        a = jnp.concatenate(parts, axis=0)
    return a


def invert(a_ref, scratch):
    columns_ref, rows_ref, row_block, column_block = scratch
    n = a_ref.shape[0]
    eye = (
        lax.broadcasted_iota(jnp.int32, (BASE, BASE), 0)
        == lax.broadcasted_iota(jnp.int32, (BASE, BASE), 1)
    ).astype(F32)

    def step(kb, carry):
        own = pl.ds(pl.multiple_of(kb * BASE, BASE), BASE)
        pivot = base_inverse(a_ref[own, own], columns_ref, rows_ref)
        row_block[:, :n] = a_ref[own, :]
        row_block[:, own] = eye
        column_block[:n, :] = a_ref[:, own]
        a_ref[:, own] = jnp.zeros((n, BASE), F32)
        q = dot6(pivot, row_block[:, :n])
        a_ref[...] = a_ref[...] - dot6(column_block[:n, :], q)
        a_ref[own, :] = q
        return carry

    lax.fori_loop(0, n // BASE, step, 0)


PAIRS = ((2, 2), (1, 2), (0, 2), (2, 3), (1, 1), (0, 1), (1, 3), (0, 0), (0, 3))


def place():
    leaf_index = lax.axis_index("leaf")
    return leaf_index // 8, (leaf_index // 2) % 4, leaf_index % 2, lax.axis_index("node")


def device(z, x, core, y):
    return ((z * 4 + x) * 2 + core, y)


class Links:
    def __init__(self, sems):
        self.sems = sems
        self.used = 0
        self.sent = []
        self.z, self.x, self.core, self.y = place()
        self.across = device(self.z, self.x, 1 - self.core, self.y)
        self.mine = {"x": self.x, "y": self.y}

    def along(self, axis, step):
        if axis == "x":
            index = lax.rem(self.x + step, 4)
            return index, device(self.z, index, self.core, self.y)
        index = lax.rem(self.y + step, 4)
        return index, device(self.z, self.x, self.core, index)

    def above(self, bit):
        return device(self.z ^ (1 << bit), self.x, self.core, self.y)

    def partners(self):
        near = [self.along(axis, step)[1] for axis in "xy" for step in (1, 2, 3)]
        return near + [self.across] + [self.above(bit) for bit in range(3)]

    def owned(self, half):
        index = self.x * 4 + self.y if half == 0 else self.y * 4 + self.x
        return pl.ds(self.core * 128 + index * 8, 8)

    def send(self, source, target, to):
        copy = pltpu.make_async_remote_copy(
            src_ref=source, dst_ref=target, send_sem=self.sems.at[self.used, 0],
            recv_sem=self.sems.at[self.used, 1], device_id=to, device_id_type=MESH,
        )
        self.used += 1
        copy.start()
        self.sent.append(copy)
        return copy


FIRST, SECOND = ("x", "y"), ("y", "x")


class Group:
    def __init__(self, links, blocks, bit, part, from_z, head=None, plane=None):
        self.links, self.blocks, self.bit = links, blocks, bit
        self.part, self.from_z, self.head, self.plane = part, from_z, head, plane
        self.pending = []

    def arrived(self):
        for copy in self.pending:
            copy.wait_recv()
        self.pending = []

    def over_cores(self):
        gram, from_core = self.plane[:2]
        links, blocks = self.links, self.blocks
        other = pl.ds((1 - links.core) * 128, 128)
        self.pending = [
            links.send(gram.at[blocks, :, other, :], from_core.at[blocks], links.across)
        ]

    def over_first(self):
        gram, from_core, one, from_one = self.plane[:4]
        links, blocks = self.links, self.blocks
        self.arrived()
        one[blocks] = gram[blocks, :, pl.ds(links.core * 128, 128), :] + from_core[blocks]
        for step in (1, 2, 3):
            for half in range(2):
                index, to = links.along(FIRST[half], step)
                source = one.at[blocks, half, pl.ds(index * 32, 32), :]
                self.pending.append(
                    links.send(source, from_one.at[step - 1, half, blocks], to)
                )

    def over_second(self):
        one, from_one, two, from_two = self.plane[2:]
        links, blocks = self.links, self.blocks
        self.arrived()
        for half in range(2):
            own = one[blocks, half, pl.ds(links.mine[FIRST[half]] * 32, 32), :]
            two[blocks, half] = (own + from_one[0, half, blocks]) + (
                from_one[1, half, blocks] + from_one[2, half, blocks]
            )
        for step in (1, 2, 3):
            for half in range(2):
                index, to = links.along(SECOND[half], step)
                source = two.at[blocks, half, pl.ds(index * 8, 8), :]
                self.pending.append(
                    links.send(source, from_two.at[step - 1, half, blocks], to)
                )

    def over_planes(self):
        links, blocks = self.links, self.blocks
        if self.plane is not None:
            two, from_two = self.plane[4:]
            self.arrived()
            for half in range(2):
                own = two[blocks, half, pl.ds(links.mine[SECOND[half]] * 8, 8), :]
                self.part[blocks, half] = (own + from_two[0, half, blocks]) + (
                    from_two[1, half, blocks] + from_two[2, half, blocks]
                )
        self.pending = [
            links.send(self.part.at[blocks], self.from_z.at[blocks], links.above(self.bit))
        ]

    def summed(self):
        self.arrived()
        return self.part[self.blocks] + self.from_z[self.blocks]

    def spread(self, half_rows, axes):
        for step in (1, 2, 3):
            for half in range(2):
                part = self.head.at[self.blocks, half, half_rows[half], :]
                self.pending.append(
                    self.links.send(part, part, self.links.along(axes[half], step)[1])
                )

    def gather_second(self):
        links = self.links
        sums = self.summed()
        for half in range(2):
            self.head[self.blocks, half, links.owned(half), :] = sums[:, half]
        self.spread([links.owned(half) for half in range(2)], SECOND)

    def gather_first(self):
        links = self.links
        self.arrived()
        self.spread(
            [pl.ds(links.core * 128 + links.mine[FIRST[half]] * 32, 32) for half in range(2)], FIRST
        )

    def gather_cores(self):
        links = self.links
        self.arrived()
        part = self.head.at[self.blocks, :, pl.ds(links.core * 128, 128), :]
        self.pending = [links.send(part, part, links.across)]


def one_hot_of(order_ref):
    n = order_ref.shape[1]
    target = lax.broadcasted_iota(jnp.int32, (n, n), 0)
    return jnp.where(target == order_ref[...], 1.0, 0.0).astype(BF16)


def whole(ref, index):
    return jnp.concatenate([ref[index, 0], ref[index, 1]], axis=1)


def plus_identity(value):
    n = value.shape[0]
    eye = lax.broadcasted_iota(jnp.int32, (n, n), 0) == lax.broadcasted_iota(jnp.int32, (n, n), 1)
    return value + jnp.where(eye, 1.0, 0.0)


def kernel(
    leaf_hbm, gens_hbm, rhs_hbm, order_hbm, out_hbm,
    inverse, gens, rhs, order, x, moved, result,
    gram, from_core, one, from_one, two, from_two,
    part2, from2, head2, part1, from1, head1, part0, from0, head0,
    small, scaled, columns_ref, rows_ref, row_block, column_block,
    in_sems, out_sem, sems,
):
    scratch = (columns_ref, rows_ref, row_block, column_block)
    links = Links(sems)
    loads = [
        pltpu.make_async_copy(source, target, in_sems.at[i])
        for i, (source, target) in enumerate(
            ((leaf_hbm, inverse), (gens_hbm, gens), (rhs_hbm, rhs), (order_hbm, order))
        )
    ]
    for load in loads:
        load.start()
    barrier = pltpu.get_barrier_semaphore()
    partners = links.partners()
    for partner in partners:
        pl.semaphore_signal(barrier, inc=1, device_id=partner, device_id_type=MESH)

    loads[0].wait()
    invert(inverse, scratch)
    for load in loads[1:]:
        load.wait()

    def apply(value):
        return dot3(inverse[...], value)

    def product(index):
        a, b = PAIRS[index]
        value = dot3(gens[a], x[b], TN)
        for half in range(2):
            gram[index, half] = value[:, half * 128 : half * 128 + 128]

    plane = (gram, from_core, one, from_one, two, from_two)
    g0, g1, g2 = (
        Group(links, blocks, 0, part2, from2, head2, plane)
        for blocks in (pl.ds(0, 1), pl.ds(1, 3), pl.ds(4, 5))
    )
    x[2] = apply(gens[2])
    product(0)
    pl.semaphore_wait(barrier, len(partners))
    g0.over_cores()
    product(1)
    product(2)
    g0.over_first()
    one_hot = one_hot_of(order)
    x[3] = apply(permute(one_hot, rhs[...], TN))
    product(3)
    g1.over_cores()
    g0.over_second()
    x[1] = apply(gens[1])
    product(4)
    product(5)
    g0.over_planes()
    g1.over_first()
    x[0] = apply(gens[0])
    product(6)
    g0.gather_second()
    product(7)
    product(8)
    g2.over_cores()
    g1.over_second()
    g0.gather_first()
    moved[2] = permute(one_hot, x[2], NN)
    g1.over_planes()
    g2.over_first()
    g0.gather_cores()
    moved[1] = permute(one_hot, x[1], NN)
    g1.gather_second()
    g2.over_second()
    moved[0] = permute(one_hot, x[0], NN)
    g1.gather_first()
    g2.over_planes()
    g1.gather_cores()
    g0.arrived()
    small[...] = plus_identity(whole(head2, 0))
    invert(small, scratch)
    g1.arrived()
    rest2 = g2.summed()

    def slices(target, index, head, a, b, scaled_b, old):
        for half in range(2):
            own = links.owned(half)
            rows = jnp.concatenate([head[a, 0, own, :], head[a, 1, own, :]], axis=1)
            update = dot3(rows, scaled_b[:, half * 128 : half * 128 + 128])
            target[index, half] = old[index, half] - update

    h0, h1, h2 = (
        Group(links, blocks, 1, part1, from1, head1)
        for blocks in (pl.ds(0, 1), pl.ds(1, 2), pl.ds(3, 2))
    )
    h2.head = None
    scaled[1] = dot3(small[...], whole(head2, 1), NT)
    slices(part1, 0, head2, 1, 1, scaled[1], rest2)
    h0.over_planes()
    scaled[2] = dot3(small[...], whole(head2, 3))
    slices(part1, 1, head2, 2, 1, scaled[1], rest2)
    slices(part1, 2, head2, 1, 3, scaled[2], rest2)
    h1.over_planes()
    scaled[0] = dot3(small[...], whole(head2, 2), NT)
    slices(part1, 3, head2, 2, 0, scaled[0], rest2)
    slices(part1, 4, head2, 2, 3, scaled[2], rest2)
    h2.over_planes()
    moved[1] = moved[1] - dot3(moved[2], scaled[1])
    h0.gather_second()
    h1.gather_second()
    moved[0] = moved[0] - dot3(moved[2], scaled[0])
    h0.gather_first()
    h1.gather_first()
    moved[3] = permute(one_hot_of(order), x[3], NN) - dot3(moved[2], scaled[2])
    h0.gather_cores()
    h1.gather_cores()
    h0.arrived()
    small[...] = plus_identity(whole(head1, 0))
    invert(small, scratch)
    h1.arrived()
    rest1 = h2.summed()

    k0, k1 = (
        Group(links, blocks, 2, part0, from0, head0) for blocks in (pl.ds(0, 1), pl.ds(1, 1))
    )
    scaled[0] = dot3(small[...], whole(head1, 1), NT)
    slices(part0, 0, head1, 1, 0, scaled[0], rest1)
    k0.over_planes()
    scaled[1] = dot3(small[...], whole(head1, 2))
    slices(part0, 1, head1, 1, 3, scaled[1], rest1)
    k1.over_planes()
    moved[0] = moved[0] - dot3(moved[1], scaled[0])
    k0.gather_second()
    k1.gather_second()
    moved[3] = moved[3] - dot3(moved[1], scaled[1])
    k0.gather_first()
    k1.gather_first()
    k0.gather_cores()
    k1.gather_cores()
    k0.arrived()
    small[...] = plus_identity(whole(head0, 0))
    invert(small, scratch)
    k1.arrived()
    coeff = dot3(small[...], whole(head0, 1))
    result[...] = moved[3] - dot3(moved[0], coeff)
    store = pltpu.make_async_copy(result, out_hbm, out_sem)
    store.start()
    for copy in links.sent:
        copy.wait_send()
    store.wait()


COPIES = 3 * (1 + 6 + 6 + 1) + 2 * 13 + 3 + 2 * 13 + 2 + 2 * 13


def per_device(leaf_blocks, generators, right_side, tree_order):
    rows, rank = leaf_blocks.shape[0], generators.shape[2]
    dma = pltpu.SemaphoreType.DMA

    def buffer(*shape):
        return pltpu.VMEM(shape, F32)

    scratch = [
        buffer(rows, rows), buffer(3, rows, rank), buffer(rows, rank), pltpu.VMEM((1, rows), jnp.int32),
        buffer(4, rows, rank), buffer(4, rows, rank), buffer(rows, rank),
        buffer(9, 2, 256, 128), buffer(9, 2, 128, 128), buffer(9, 2, 128, 128),
        buffer(3, 2, 9, 32, 128), buffer(9, 2, 32, 128), buffer(3, 2, 9, 8, 128),
        buffer(9, 2, 8, 128), buffer(9, 2, 8, 128), buffer(4, 2, 256, 128),
        buffer(5, 2, 8, 128), buffer(5, 2, 8, 128), buffer(3, 2, 256, 128),
        buffer(2, 2, 8, 128), buffer(2, 2, 8, 128), buffer(2, 2, 256, 128),
        buffer(rank, rank), buffer(3, rank, rank),
        buffer(2, 8, 8, BASE), buffer(2, 8, BASE), buffer(BASE, rows), buffer(rows, BASE),
        dma((4,)), dma(()), dma((COPIES, 2)),
    ]
    hbm = pl.BlockSpec(memory_space=pltpu.MemorySpace.HBM)
    return pl.pallas_call(
        kernel,
        out_shape=jax.ShapeDtypeStruct(right_side.shape, F32),
        in_specs=[hbm] * 4,
        out_specs=hbm,
        scratch_shapes=scratch,
        compiler_params=pltpu.CompilerParams(
            collective_id=0, has_side_effects=True, vmem_limit_bytes=VMEM_LIMIT
        ),
        name="solve",
    )(leaf_blocks, generators, right_side, tree_order)


def solution(mesh):
    return jax.shard_map(
        per_device,
        mesh=mesh,
        in_specs=(
            P(("leaf", "node"), None),
            P(None, ("leaf", "node"), None),
            P(("leaf", "node"), None),
            P(("leaf", "node"), None),
        ),
        out_specs=P(("leaf", "node"), None),
        check_vma=False,
    )
```

```python
import functools

import jax
import jax.numpy as jnp
from jax import lax
from jax.experimental import pallas as pl
from jax.experimental.pallas import tpu as pltpu
from jax.sharding import PartitionSpec as P

F32 = jnp.float32
BF16 = jnp.bfloat16
MESH = pl.DeviceIdType.MESH
NN = (((1,), (0,)), ((), ()))
NT = (((1,), (1,)), ((), ()))
TN = (((0,), (0,)), ((), ()))
BASE = 128
VMEM_LIMIT = 64 * 2**20 - 2**17


def split(value):
    high = value.astype(BF16)
    return high, (value - high.astype(F32)).astype(BF16)


def dot3(left, right, dims=NN):
    left_high, left_low = split(left)
    right_high, right_low = split(right)
    one = functools.partial(lax.dot_general, dimension_numbers=dims, preferred_element_type=F32)
    return one(left_high, right_high) + (one(left_high, right_low) + one(left_low, right_high))


def dot6(left, right, dims=NN):
    return lax.dot_general(
        left, right, dims, precision=lax.Precision.HIGHEST, preferred_element_type=F32
    )


def permute(one_hot, value, dims):
    high = value.astype(BF16)
    rest = value - high.astype(F32)
    middle = rest.astype(BF16)
    low = (rest - middle.astype(F32)).astype(BF16)
    one = functools.partial(lax.dot_general, dimension_numbers=dims, preferred_element_type=F32)
    return one(one_hot, high) + (one(one_hot, middle) + one(one_hot, low))


def ldl_factor(p):
    p = [list(row) for row in p]
    n = len(p)
    lower = [[None] * n for _ in range(n)]
    pivots = []
    for k in range(n):
        r = 1.0 / p[k][k]
        pivots.append(r)
        raw = [p[i][k] for i in range(n)] if k == 0 else [p[i][k] if i > k else None for i in range(n)]
        for i in range(k + 1, n):
            for j in range(k + 1, i + 1):
                p[i][j] = p[i][j] - r * (raw[i] * raw[j])
        for i in range(k + 1, n):
            lower[i][k] = raw[i] * r
    return lower, pivots


def ldl_solve(lower, pivots, rows):
    n = len(rows)
    y = list(rows)
    for k in range(n):
        for i in range(k + 1, n):
            y[i] = y[i] - lower[i][k] * y[k]
    z = [y[i] * pivots[i] for i in range(n)]
    for k in range(n - 1, -1, -1):
        for i in range(k):
            z[i] = z[i] - lower[k][i] * z[k]
    return z


def base_inverse(a, columns_ref, rows_ref):
    n = a.shape[0]
    lane8 = lax.broadcasted_iota(jnp.int32, (8, n), 1)
    sub8 = lax.broadcasted_iota(jnp.int32, (8, n), 0)
    lane = lax.broadcasted_iota(jnp.int32, (n, n), 1)
    for kb in range(n // 8):
        k = 8 * kb
        slot = kb % 2
        own = a[k : k + 8, :]
        for j in range(8):
            columns_ref[slot, j] = jnp.broadcast_to(own[:, k + j : k + j + 1], (8, n))
        inside = (lane8 >= k) & (lane8 < k + 8)
        rows_ref[slot] = jnp.where(inside, jnp.where(lane8 == sub8 + k, 1.0, 0.0), own)
        p = [
            [jnp.broadcast_to(columns_ref[slot, j, i : i + 1, :], (8, n)) for j in range(i + 1)]
            for i in range(8)
        ]
        rows = [jnp.broadcast_to(rows_ref[slot, i : i + 1, :], (8, n)) for i in range(8)]
        q = ldl_solve(*ldl_factor(p), rows)
        own = q[0]
        for j in range(1, 8):
            own = jnp.where(sub8 == j, q[j], own)
        rest = jnp.where((lane >= k) & (lane < k + 8), 0.0, a)
        terms = [
            jnp.broadcast_to(a[:, k + j : k + j + 1], (n, n))
            * jnp.broadcast_to(q[j][0:1, :], (n, n))
            for j in range(8)
        ]
        while len(terms) > 1:
            terms = [terms[i] + terms[i + 1] for i in range(0, len(terms), 2)]
        rest = rest - terms[0]
        parts = [rest[:k]] if k else []
        parts.append(own)
        if k + 8 < n:
            parts.append(rest[k + 8 :])
        a = jnp.concatenate(parts, axis=0)
    return a


def invert(a_ref, scratch, hooks=None):
    columns_ref, rows_ref, row_block, column_block = scratch
    n = a_ref.shape[0]
    eye = (
        lax.broadcasted_iota(jnp.int32, (BASE, BASE), 0)
        == lax.broadcasted_iota(jnp.int32, (BASE, BASE), 1)
    ).astype(F32)

    def step(own, hook):
        pivot = base_inverse(a_ref[own, own], columns_ref, rows_ref)
        hook()
        row_block[:, :n] = a_ref[own, :]
        row_block[:, own] = eye
        column_block[:n, :] = a_ref[:, own]
        a_ref[:, own] = jnp.zeros((n, BASE), F32)
        q = dot6(pivot, row_block[:, :n])
        a_ref[...] = a_ref[...] - dot6(column_block[:n, :], q)
        a_ref[own, :] = q

    if hooks is None:
        def body(kb, carry):
            step(pl.ds(pl.multiple_of(kb * BASE, BASE), BASE), lambda: None)
            return carry

        lax.fori_loop(0, n // BASE, body, 0)
        return
    for kb in range(n // BASE):
        step(pl.ds(kb * BASE, BASE), hooks[2 * kb])
        hooks[2 * kb + 1]()


PAIRS = ((2, 2), (1, 2), (0, 2), (2, 3), (1, 1), (0, 1), (1, 3), (0, 0), (0, 3))


def place():
    leaf_index = lax.axis_index("leaf")
    return leaf_index // 8, (leaf_index // 2) % 4, leaf_index % 2, lax.axis_index("node")


def device(z, x, core, y):
    return ((z * 4 + x) * 2 + core, y)


class Links:
    def __init__(self, sems):
        self.sems = sems
        self.used = 0
        self.sent = []
        self.z, self.x, self.core, self.y = place()
        self.across = device(self.z, self.x, 1 - self.core, self.y)
        self.mine = {"x": self.x, "y": self.y}

    def along(self, axis, step):
        if axis == "x":
            index = lax.rem(self.x + step, 4)
            return index, device(self.z, index, self.core, self.y)
        index = lax.rem(self.y + step, 4)
        return index, device(self.z, self.x, self.core, index)

    def above(self, bit):
        return device(self.z ^ (1 << bit), self.x, self.core, self.y)

    def partners(self):
        near = [self.along(axis, step)[1] for axis in "xy" for step in (1, 2, 3)]
        return near + [self.across] + [self.above(bit) for bit in range(3)]

    def owned(self, half):
        index = self.x * 4 + self.y if half == 0 else self.y * 4 + self.x
        return pl.ds(self.core * 128 + index * 8, 8)

    def send(self, source, target, to):
        copy = pltpu.make_async_remote_copy(
            src_ref=source, dst_ref=target, send_sem=self.sems.at[self.used, 0],
            recv_sem=self.sems.at[self.used, 1], device_id=to, device_id_type=MESH,
        )
        self.used += 1
        copy.start()
        self.sent.append(copy)
        return copy


FIRST, SECOND = ("x", "y"), ("y", "x")


class Group:
    def __init__(self, links, blocks, bit, part, from_z, head=None, plane=None):
        self.links, self.blocks, self.bit = links, blocks, bit
        self.part, self.from_z, self.head, self.plane = part, from_z, head, plane
        self.pending = []

    def arrived(self):
        for copy in self.pending:
            copy.wait_recv()
        self.pending = []

    def over_cores(self):
        gram, from_core = self.plane[:2]
        links, blocks = self.links, self.blocks
        other = pl.ds((1 - links.core) * 128, 128)
        self.pending = [
            links.send(gram.at[blocks, :, other, :], from_core.at[blocks], links.across)
        ]

    def over_first(self):
        gram, from_core, one, from_one = self.plane[:4]
        links, blocks = self.links, self.blocks
        self.arrived()
        one[blocks] = gram[blocks, :, pl.ds(links.core * 128, 128), :] + from_core[blocks]
        for step in (1, 2, 3):
            for half in range(2):
                index, to = links.along(FIRST[half], step)
                source = one.at[blocks, half, pl.ds(index * 32, 32), :]
                self.pending.append(
                    links.send(source, from_one.at[step - 1, half, blocks], to)
                )

    def over_second(self):
        one, from_one, two, from_two = self.plane[2:]
        links, blocks = self.links, self.blocks
        self.arrived()
        for half in range(2):
            own = one[blocks, half, pl.ds(links.mine[FIRST[half]] * 32, 32), :]
            two[blocks, half] = (own + from_one[0, half, blocks]) + (
                from_one[1, half, blocks] + from_one[2, half, blocks]
            )
        for step in (1, 2, 3):
            for half in range(2):
                index, to = links.along(SECOND[half], step)
                source = two.at[blocks, half, pl.ds(index * 8, 8), :]
                self.pending.append(
                    links.send(source, from_two.at[step - 1, half, blocks], to)
                )

    def over_planes(self):
        links, blocks = self.links, self.blocks
        if self.plane is not None:
            two, from_two = self.plane[4:]
            self.arrived()
            for half in range(2):
                own = two[blocks, half, pl.ds(links.mine[SECOND[half]] * 8, 8), :]
                self.part[blocks, half] = (own + from_two[0, half, blocks]) + (
                    from_two[1, half, blocks] + from_two[2, half, blocks]
                )
        self.pending = [
            links.send(self.part.at[blocks], self.from_z.at[blocks], links.above(self.bit))
        ]

    def summed(self):
        self.arrived()
        return self.part[self.blocks] + self.from_z[self.blocks]

    def spread(self, half_rows, axes):
        for step in (1, 2, 3):
            for half in range(2):
                part = self.head.at[self.blocks, half, half_rows[half], :]
                self.pending.append(
                    self.links.send(part, part, self.links.along(axes[half], step)[1])
                )

    def gather_second(self):
        links = self.links
        sums = self.summed()
        for half in range(2):
            self.head[self.blocks, half, links.owned(half), :] = sums[:, half]
        self.spread([links.owned(half) for half in range(2)], SECOND)

    def gather_first(self):
        links = self.links
        self.arrived()
        self.spread(
            [pl.ds(links.core * 128 + links.mine[FIRST[half]] * 32, 32) for half in range(2)], FIRST
        )

    def gather_cores(self):
        links = self.links
        self.arrived()
        part = self.head.at[self.blocks, :, pl.ds(links.core * 128, 128), :]
        self.pending = [links.send(part, part, links.across)]


def one_hot_of(order_ref):
    n = order_ref.shape[1]
    target = lax.broadcasted_iota(jnp.int32, (n, n), 0)
    return jnp.where(target == order_ref[...], 1.0, 0.0).astype(BF16)


def whole(ref, index):
    return jnp.concatenate([ref[index, 0], ref[index, 1]], axis=1)


def plus_identity(value):
    n = value.shape[0]
    eye = lax.broadcasted_iota(jnp.int32, (n, n), 0) == lax.broadcasted_iota(jnp.int32, (n, n), 1)
    return value + jnp.where(eye, 1.0, 0.0)


def nothing():
    pass


def kernel(
    leaf_hbm, gens_hbm, rhs_hbm, order_hbm, out_hbm,
    inverse, gens, rhs, order, x, moved, result,
    gram, from_core, one, from_one, two, from_two,
    part2, from2, head2, part1, from1, head1, part0, from0, head0,
    small, scaled, columns_ref, rows_ref, row_block, column_block,
    in_sems, out_sem, sems,
):
    scratch = (columns_ref, rows_ref, row_block, column_block)
    links = Links(sems)
    loads = [
        pltpu.make_async_copy(source, target, in_sems.at[i])
        for i, (source, target) in enumerate(
            ((leaf_hbm, inverse), (gens_hbm, gens), (rhs_hbm, rhs), (order_hbm, order))
        )
    ]
    for load in loads:
        load.start()
    barrier = pltpu.get_barrier_semaphore()
    partners = links.partners()
    for partner in partners:
        pl.semaphore_signal(barrier, inc=1, device_id=partner, device_id_type=MESH)

    loads[0].wait()
    invert(inverse, scratch)
    for load in loads[1:]:
        load.wait()

    def apply(value):
        return dot3(inverse[...], value)

    def product(index):
        a, b = PAIRS[index]
        value = dot3(gens[a], x[b], TN)
        for half in range(2):
            gram[index, half] = value[:, half * 128 : half * 128 + 128]

    plane = (gram, from_core, one, from_one, two, from_two)
    g0, g1, g2 = (
        Group(links, blocks, 0, part2, from2, head2, plane)
        for blocks in (pl.ds(0, 1), pl.ds(1, 3), pl.ds(4, 5))
    )
    x[2] = apply(gens[2])
    product(0)
    pl.semaphore_wait(barrier, len(partners))
    g0.over_cores()
    product(1)
    g0.over_first()
    one_hot = one_hot_of(order)
    product(2)
    x[3] = apply(permute(one_hot, rhs[...], TN))
    g0.over_second()
    product(3)
    g1.over_cores()
    x[1] = apply(gens[1])
    g0.over_planes()
    g1.over_first()
    product(4)
    product(5)
    product(6)
    g0.gather_second()
    g1.over_second()
    x[0] = apply(gens[0])
    product(7)
    g0.gather_first()
    g1.over_planes()
    product(8)
    g2.over_cores()
    moved[2] = permute(one_hot, x[2], NN)
    g0.gather_cores()
    g1.gather_second()
    g2.over_first()
    g0.arrived()
    small[...] = plus_identity(whole(head2, 0))

    def hook_two():
        g1.gather_first()
        g2.over_second()

    def hook_three():
        g1.gather_cores()
        g2.over_planes()

    invert(small, scratch, (hook_two, nothing, hook_three, nothing))

    def slices(target, index, head, a, scaled_b, old):
        for half in range(2):
            own = links.owned(half)
            rows = jnp.concatenate([head[a, 0, own, :], head[a, 1, own, :]], axis=1)
            update = dot3(rows, scaled_b[:, half * 128 : half * 128 + 128])
            target[index, half] = old[index, half] - update

    h0, h1, h2 = (
        Group(links, blocks, 1, part1, from1, head1)
        for blocks in (pl.ds(0, 1), pl.ds(1, 2), pl.ds(3, 2))
    )
    g1.arrived()
    scaled[1] = dot3(small[...], whole(head2, 1), NT)
    rest2 = g2.summed()
    slices(part1, 0, head2, 1, scaled[1], rest2)
    h0.over_planes()
    scaled[2] = dot3(small[...], whole(head2, 3))
    slices(part1, 1, head2, 2, scaled[1], rest2)
    slices(part1, 2, head2, 1, scaled[2], rest2)
    h1.over_planes()
    scaled[0] = dot3(small[...], whole(head2, 2), NT)
    slices(part1, 3, head2, 2, scaled[0], rest2)
    slices(part1, 4, head2, 2, scaled[2], rest2)
    h2.over_planes()
    h0.gather_second()
    moved[1] = permute(one_hot_of(order), x[1], NN) - dot3(moved[2], scaled[1])
    h0.gather_first()
    moved[0] = permute(one_hot_of(order), x[0], NN) - dot3(moved[2], scaled[0])
    h0.gather_cores()
    h1.gather_second()
    h0.arrived()
    small[...] = plus_identity(whole(head1, 0))
    invert(small, scratch, (h1.gather_first, nothing, h1.gather_cores, nothing))

    k0, k1 = (
        Group(links, blocks, 2, part0, from0, head0) for blocks in (pl.ds(0, 1), pl.ds(1, 1))
    )
    h1.arrived()
    scaled[0] = dot3(small[...], whole(head1, 1), NT)
    rest1 = h2.summed()
    slices(part0, 0, head1, 1, scaled[0], rest1)
    k0.over_planes()
    scaled[1] = dot3(small[...], whole(head1, 2))
    slices(part0, 1, head1, 1, scaled[1], rest1)
    k1.over_planes()
    moved[3] = permute(one_hot_of(order), x[3], NN) - dot3(moved[2], scaled[2])
    k0.gather_second()
    moved[0] = moved[0] - dot3(moved[1], scaled[0])
    k0.gather_first()
    moved[3] = moved[3] - dot3(moved[1], scaled[1])
    k0.gather_cores()
    k1.gather_second()
    k0.arrived()
    small[...] = plus_identity(whole(head0, 0))
    invert(small, scratch, (k1.gather_first, nothing, k1.gather_cores, nothing))
    k1.arrived()
    coeff = dot3(small[...], whole(head0, 1))
    result[...] = moved[3] - dot3(moved[0], coeff)
    store = pltpu.make_async_copy(result, out_hbm, out_sem)
    store.start()
    for copy in links.sent:
        copy.wait_send()
    store.wait()


COPIES = 3 * (1 + 6 + 6 + 1) + 2 * 13 + 3 + 2 * 13 + 2 + 2 * 13


def per_device(leaf_blocks, generators, right_side, tree_order):
    rows, rank = leaf_blocks.shape[0], generators.shape[2]
    dma = pltpu.SemaphoreType.DMA

    def buffer(*shape):
        return pltpu.VMEM(shape, F32)

    scratch = [
        buffer(rows, rows), buffer(3, rows, rank), buffer(rows, rank), pltpu.VMEM((1, rows), jnp.int32),
        buffer(4, rows, rank), buffer(4, rows, rank), buffer(rows, rank),
        buffer(9, 2, 256, 128), buffer(9, 2, 128, 128), buffer(9, 2, 128, 128),
        buffer(3, 2, 9, 32, 128), buffer(9, 2, 32, 128), buffer(3, 2, 9, 8, 128),
        buffer(9, 2, 8, 128), buffer(9, 2, 8, 128), buffer(4, 2, 256, 128),
        buffer(5, 2, 8, 128), buffer(5, 2, 8, 128), buffer(3, 2, 256, 128),
        buffer(2, 2, 8, 128), buffer(2, 2, 8, 128), buffer(2, 2, 256, 128),
        buffer(rank, rank), buffer(3, rank, rank),
        buffer(2, 8, 8, BASE), buffer(2, 8, BASE), buffer(BASE, rows), buffer(rows, BASE),
        dma((4,)), dma(()), dma((COPIES, 2)),
    ]
    hbm = pl.BlockSpec(memory_space=pltpu.MemorySpace.HBM)
    return pl.pallas_call(
        kernel,
        out_shape=jax.ShapeDtypeStruct(right_side.shape, F32),
        in_specs=[hbm] * 4,
        out_specs=hbm,
        scratch_shapes=scratch,
        compiler_params=pltpu.CompilerParams(
            collective_id=0, has_side_effects=True, vmem_limit_bytes=VMEM_LIMIT
        ),
        name="solve",
    )(leaf_blocks, generators, right_side, tree_order)


def solution(mesh):
    return jax.shard_map(
        per_device,
        mesh=mesh,
        in_specs=(
            P(("leaf", "node"), None),
            P(None, ("leaf", "node"), None),
            P(("leaf", "node"), None),
            P(("leaf", "node"), None),
        ),
        out_specs=P(("leaf", "node"), None),
        check_vma=False,
    )
```

```python
import functools

import jax
import jax.numpy as jnp
from jax import lax
from jax.experimental import pallas as pl
from jax.experimental.pallas import tpu as pltpu
from jax.sharding import PartitionSpec as P

F32 = jnp.float32
BF16 = jnp.bfloat16
MESH = pl.DeviceIdType.MESH
NN = (((1,), (0,)), ((), ()))
NT = (((1,), (1,)), ((), ()))
TN = (((0,), (0,)), ((), ()))
BASE = 128
VMEM_LIMIT = 64 * 2**20 - 3 * 2**18


def split(value):
    high = value.astype(BF16)
    return high, (value - high.astype(F32)).astype(BF16)


def dot3(left, right, dims=NN):
    left_high, left_low = split(left)
    right_high, right_low = split(right)
    one = functools.partial(lax.dot_general, dimension_numbers=dims, preferred_element_type=F32)
    return one(left_high, right_high) + (one(left_high, right_low) + one(left_low, right_high))


def dot6(left, right, dims=NN):
    return lax.dot_general(
        left, right, dims, precision=lax.Precision.HIGHEST, preferred_element_type=F32
    )


def permute(one_hot, value, dims):
    high = value.astype(BF16)
    rest = value - high.astype(F32)
    middle = rest.astype(BF16)
    low = (rest - middle.astype(F32)).astype(BF16)
    one = functools.partial(lax.dot_general, dimension_numbers=dims, preferred_element_type=F32)
    return one(one_hot, high) + (one(one_hot, middle) + one(one_hot, low))


def ldl_factor(p):
    p = [list(row) for row in p]
    n = len(p)
    lower = [[None] * n for _ in range(n)]
    pivots = []
    for k in range(n):
        r = 1.0 / p[k][k]
        pivots.append(r)
        raw = [p[i][k] for i in range(n)] if k == 0 else [p[i][k] if i > k else None for i in range(n)]
        for i in range(k + 1, n):
            for j in range(k + 1, i + 1):
                p[i][j] = p[i][j] - r * (raw[i] * raw[j])
        for i in range(k + 1, n):
            lower[i][k] = raw[i] * r
    return lower, pivots


def ldl_solve(lower, pivots, rows):
    n = len(rows)
    y = list(rows)
    for k in range(n):
        for i in range(k + 1, n):
            y[i] = y[i] - lower[i][k] * y[k]
    z = [y[i] * pivots[i] for i in range(n)]
    for k in range(n - 1, -1, -1):
        for i in range(k):
            z[i] = z[i] - lower[k][i] * z[k]
    return z


def base_inverse(a, columns_ref, rows_ref):
    n = a.shape[0]
    lane8 = lax.broadcasted_iota(jnp.int32, (8, n), 1)
    sub8 = lax.broadcasted_iota(jnp.int32, (8, n), 0)
    lane = lax.broadcasted_iota(jnp.int32, (n, n), 1)
    for kb in range(n // 8):
        k = 8 * kb
        slot = kb % 2
        own = a[k : k + 8, :]
        for j in range(8):
            column = jnp.sum(jnp.where(lane8 == k + j, own, 0.0), axis=1, keepdims=True)
            columns_ref[slot, j] = jnp.broadcast_to(column, (8, n))
        inside = (lane8 >= k) & (lane8 < k + 8)
        rows_ref[slot] = jnp.where(inside, jnp.where(lane8 == sub8 + k, 1.0, 0.0), own)
        p = [
            [jnp.broadcast_to(columns_ref[slot, j, i : i + 1, :], (8, n)) for j in range(i + 1)]
            for i in range(8)
        ]
        rows = [jnp.broadcast_to(rows_ref[slot, i : i + 1, :], (8, n)) for i in range(8)]
        q = ldl_solve(*ldl_factor(p), rows)
        own = q[0]
        for j in range(1, 8):
            own = jnp.where(sub8 == j, q[j], own)
        rest = jnp.where((lane >= k) & (lane < k + 8), 0.0, a)
        terms = [
            jnp.broadcast_to(a[:, k + j : k + j + 1], (n, n))
            * jnp.broadcast_to(q[j][0:1, :], (n, n))
            for j in range(8)
        ]
        while len(terms) > 1:
            terms = [terms[i] + terms[i + 1] for i in range(0, len(terms), 2)]
        rest = rest - terms[0]
        parts = [rest[:k]] if k else []
        parts.append(own)
        if k + 8 < n:
            parts.append(rest[k + 8 :])
        a = jnp.concatenate(parts, axis=0)
    return a


def invert(a_ref, scratch, hooks=None):
    columns_ref, rows_ref, row_block, column_block = scratch
    n = a_ref.shape[0]
    eye = (
        lax.broadcasted_iota(jnp.int32, (BASE, BASE), 0)
        == lax.broadcasted_iota(jnp.int32, (BASE, BASE), 1)
    ).astype(F32)

    def step(own, hook):
        pivot = base_inverse(a_ref[own, own], columns_ref, rows_ref)
        hook()
        row_block[:, :n] = a_ref[own, :]
        row_block[:, own] = eye
        column_block[:n, :] = a_ref[:, own]
        a_ref[:, own] = jnp.zeros((n, BASE), F32)
        q = dot6(pivot, row_block[:, :n])
        a_ref[...] = a_ref[...] - dot6(column_block[:n, :], q)
        a_ref[own, :] = q

    if hooks is None:
        def body(kb, carry):
            step(pl.ds(pl.multiple_of(kb * BASE, BASE), BASE), lambda: None)
            return carry

        lax.fori_loop(0, n // BASE, body, 0)
        return
    for kb in range(n // BASE):
        step(pl.ds(kb * BASE, BASE), hooks[2 * kb])
        hooks[2 * kb + 1]()


PAIRS = ((2, 2), (1, 2), (0, 2), (2, 3), (1, 1), (0, 1), (1, 3), (0, 0), (0, 3))


def place():
    leaf_index = lax.axis_index("leaf")
    return leaf_index // 8, (leaf_index // 2) % 4, leaf_index % 2, lax.axis_index("node")


def device(z, x, core, y):
    return ((z * 4 + x) * 2 + core, y)


OTHERS = tuple((right, up) for right in range(4) for up in range(4) if right or up)


class Links:
    def __init__(self, sems):
        self.sems = sems
        self.used = 0
        self.sent = []
        self.z, self.x, self.core, self.y = place()
        self.across = device(self.z, self.x, 1 - self.core, self.y)

    def along(self, axis, step):
        if axis == "x":
            index = lax.rem(self.x + step, 4)
            return index, device(self.z, index, self.core, self.y)
        index = lax.rem(self.y + step, 4)
        return index, device(self.z, self.x, self.core, index)

    def above(self, bit):
        return device(self.z ^ (1 << bit), self.x, self.core, self.y)

    def partners(self):
        near = [self.at(right, up)[2] for right, up in OTHERS]
        return near + [self.across] + [self.above(bit) for bit in range(3)]

    def at(self, right, up):
        x, y = lax.rem(self.x + right, 4), lax.rem(self.y + up, 4)
        return x, y, device(self.z, x, self.core, y)

    def send(self, source, target, to):
        copy = pltpu.make_async_remote_copy(
            src_ref=source, dst_ref=target, send_sem=self.sems.at[self.used, 0],
            recv_sem=self.sems.at[self.used, 1], device_id=to, device_id_type=MESH,
        )
        self.used += 1
        copy.start()
        self.sent.append(copy)
        return copy


class Group:
    def __init__(self, links, blocks, bit, part, from_z, head=None, plane=None):
        self.links, self.blocks, self.bit = links, blocks, bit
        self.part, self.from_z, self.head, self.plane = part, from_z, head, plane
        self.from_plane = None
        self.pending = []

    def arrived(self):
        for copy in self.pending:
            copy.wait_recv()
        self.pending = []

    def over_cores(self):
        gram, from_core = self.plane[:2]
        links, blocks = self.links, self.blocks
        source = gram.at[blocks, :, 1 - links.core]
        self.pending = [links.send(source, from_core.at[blocks], links.across)]

    def add_cores(self):
        gram, from_core, one = self.plane[:3]
        blocks = self.blocks
        self.arrived()
        one[blocks] = gram[blocks, :, self.links.core] + from_core[blocks]

    def over_plane(self, from_plane):
        one = self.plane[2]
        links, blocks = self.links, self.blocks
        self.add_cores()
        for slot, (right, up) in enumerate(OTHERS):
            x, y, to = links.at(right, up)
            source = one.at[blocks, :, x, y]
            self.pending.append(links.send(source, from_plane.at[slot], to))
        self.from_plane = from_plane

    def over_first(self):
        one, from_one = self.plane[2:4]
        links, blocks = self.links, self.blocks
        self.add_cores()
        for step in (1, 2, 3):
            x, to_x = links.along("x", step)
            y, to_y = links.along("y", step)
            self.pending += [
                links.send(one.at[blocks, 0, x], from_one.at[step - 1, 0, blocks], to_x),
                links.send(one.at[blocks, 1, :, y], from_one.at[step - 1, 1, blocks], to_y),
            ]

    def over_second(self):
        one, from_one, two, from_two = self.plane[2:]
        links, blocks = self.links, self.blocks
        self.arrived()
        for half, own in enumerate((one[blocks, 0, links.x], one[blocks, 1, :, links.y])):
            two[blocks, half] = (own + from_one[0, half, blocks]) + (
                from_one[1, half, blocks] + from_one[2, half, blocks]
            )
        for step in (1, 2, 3):
            x, to_x = links.along("x", step)
            y, to_y = links.along("y", step)
            self.pending += [
                links.send(two.at[blocks, 0, y], from_two.at[step - 1, 0, blocks], to_y),
                links.send(two.at[blocks, 1, x], from_two.at[step - 1, 1, blocks], to_x),
            ]

    def over_planes(self):
        links, blocks = self.links, self.blocks
        self.arrived()
        if self.from_plane is not None:
            terms = [self.plane[2][blocks, :, links.x, links.y]]
            terms += [self.from_plane[slot] for slot in range(len(OTHERS))]
            while len(terms) > 1:
                terms = [terms[i] + terms[i + 1] for i in range(0, len(terms), 2)]
            self.part[blocks] = terms[0]
        elif self.plane is not None:
            two, from_two = self.plane[4:]
            for half, own in enumerate((two[blocks, 0, links.y], two[blocks, 1, links.x])):
                self.part[blocks, half] = (own + from_two[0, half, blocks]) + (
                    from_two[1, half, blocks] + from_two[2, half, blocks]
                )
        self.pending = [
            links.send(self.part.at[blocks], self.from_z.at[blocks], links.above(self.bit))
        ]

    def summed(self):
        self.arrived()
        return self.part[self.blocks] + self.from_z[self.blocks]

    def spread(self, part, to):
        self.pending.append(self.links.send(part, part, to))

    def gather_plane(self):
        links = self.links
        self.head[self.blocks, :, links.core, links.x, links.y] = self.summed()
        for right, up in OTHERS:
            part = self.head.at[self.blocks, :, links.core, links.x, links.y]
            self.spread(part, links.at(right, up)[2])

    def gather_second(self):
        links = self.links
        self.head[self.blocks, :, links.core, links.x, links.y] = self.summed()
        for step in (1, 2, 3):
            for half, axis in enumerate("yx"):
                part = self.head.at[self.blocks, half, links.core, links.x, links.y]
                self.spread(part, links.along(axis, step)[1])

    def gather_first(self):
        links = self.links
        self.arrived()
        for step in (1, 2, 3):
            self.spread(self.head.at[self.blocks, 0, links.core, links.x], links.along("x", step)[1])
            self.spread(
                self.head.at[self.blocks, 1, links.core, :, links.y], links.along("y", step)[1]
            )

    def gather_cores(self):
        links = self.links
        self.arrived()
        self.spread(self.head.at[self.blocks, :, links.core], links.across)


def one_hot_of(order_ref):
    n = order_ref.shape[1]
    target = lax.broadcasted_iota(jnp.int32, (n, n), 0)
    return jnp.where(target == order_ref[...], 1.0, 0.0).astype(BF16)


def whole(ref, index):
    return jnp.concatenate([ref[index, half].reshape(256, 128) for half in range(2)], axis=1)


def plus_identity(value):
    n = value.shape[0]
    eye = lax.broadcasted_iota(jnp.int32, (n, n), 0) == lax.broadcasted_iota(jnp.int32, (n, n), 1)
    return value + jnp.where(eye, 1.0, 0.0)


def nothing():
    pass


def kernel(
    leaf_hbm, gens_hbm, rhs_hbm, order_hbm, out_hbm,
    inverse, gens, rhs, order, x, moved, result,
    gram, from_core, one, from_one, two, from_two, from_plane,
    part2, from2, head2, part1, from1, head1, part0, from0, head0,
    small, scaled, columns_ref, rows_ref, row_block, column_block,
    in_sems, out_sem, sems,
):
    scratch = (columns_ref, rows_ref, row_block, column_block)
    links = Links(sems)
    loads = [
        pltpu.make_async_copy(source, target, in_sems.at[i])
        for i, (source, target) in enumerate(
            ((leaf_hbm, inverse), (gens_hbm, gens), (rhs_hbm, rhs), (order_hbm, order))
        )
    ]
    for load in loads:
        load.start()
    barrier = pltpu.get_barrier_semaphore()
    partners = links.partners()
    for partner in partners:
        pl.semaphore_signal(barrier, inc=1, device_id=partner, device_id_type=MESH)

    loads[0].wait()
    invert(inverse, scratch)
    for load in loads[1:]:
        load.wait()

    def apply(value):
        return dot3(inverse[...], value)

    def product(index):
        a, b = PAIRS[index]
        value = dot3(gens[a], x[b], TN)
        for half in range(2):
            columns = value[:, half * 128 : half * 128 + 128]
            gram[index, half] = columns.reshape(gram.shape[2:])

    plane = (gram, from_core, one, from_one, two, from_two)
    g0, g1, g2 = (
        Group(links, blocks, 0, part2, from2, head2, plane)
        for blocks in (pl.ds(0, 1), pl.ds(1, 3), pl.ds(4, 5))
    )
    x[2] = apply(gens[2])
    product(0)
    pl.semaphore_wait(barrier, len(partners))
    g0.over_cores()
    product(1)
    g0.over_plane(from_plane)
    one_hot = one_hot_of(order)
    product(2)
    x[3] = apply(permute(one_hot, rhs[...], TN))
    product(3)
    g1.over_cores()
    x[1] = apply(gens[1])
    g0.over_planes()
    g1.over_first()
    product(4)
    product(5)
    g0.gather_plane()
    g1.over_second()
    x[0] = apply(gens[0])
    product(6)
    product(7)
    product(8)
    g2.over_cores()
    g1.over_planes()
    g0.gather_cores()
    moved[2] = permute(one_hot, x[2], NN)
    g1.gather_second()
    g2.over_first()
    g0.arrived()
    small[...] = plus_identity(whole(head2, 0))

    def hook_two():
        g1.gather_first()
        g2.over_second()

    def hook_three():
        g1.gather_cores()
        g2.over_planes()

    invert(small, scratch, (hook_two, nothing, hook_three, nothing))

    def slices(target, index, head, a, scaled_b, old):
        rows = jnp.concatenate(
            [head[a, half, links.core, links.x, links.y] for half in range(2)], axis=1
        )
        for half in range(2):
            update = dot3(rows, scaled_b[:, half * 128 : half * 128 + 128])
            target[index, half] = old[index, half] - update

    h0, h1, h2 = (
        Group(links, blocks, 1, part1, from1, head1)
        for blocks in (pl.ds(0, 1), pl.ds(1, 2), pl.ds(3, 2))
    )
    g1.arrived()
    scaled[1] = dot3(small[...], whole(head2, 1), NT)
    rest2 = g2.summed()
    slices(part1, 0, head2, 1, scaled[1], rest2)
    h0.over_planes()
    scaled[2] = dot3(small[...], whole(head2, 3))
    slices(part1, 1, head2, 2, scaled[1], rest2)
    slices(part1, 2, head2, 1, scaled[2], rest2)
    h1.over_planes()
    scaled[0] = dot3(small[...], whole(head2, 2), NT)
    slices(part1, 3, head2, 2, scaled[0], rest2)
    slices(part1, 4, head2, 2, scaled[2], rest2)
    h2.over_planes()
    h0.gather_plane()
    moved[1] = permute(one_hot_of(order), x[1], NN) - dot3(moved[2], scaled[1])
    moved[0] = permute(one_hot_of(order), x[0], NN) - dot3(moved[2], scaled[0])
    h1.gather_second()
    h0.gather_cores()
    h0.arrived()
    small[...] = plus_identity(whole(head1, 0))
    invert(small, scratch, (h1.gather_first, nothing, h1.gather_cores, nothing))

    k0, k1 = (
        Group(links, blocks, 2, part0, from0, head0) for blocks in (pl.ds(0, 1), pl.ds(1, 1))
    )
    h1.arrived()
    scaled[0] = dot3(small[...], whole(head1, 1), NT)
    rest1 = h2.summed()
    slices(part0, 0, head1, 1, scaled[0], rest1)
    k0.over_planes()
    scaled[1] = dot3(small[...], whole(head1, 2))
    slices(part0, 1, head1, 1, scaled[1], rest1)
    k1.over_planes()
    moved[3] = permute(one_hot_of(order), x[3], NN) - dot3(moved[2], scaled[2])
    k0.gather_plane()
    moved[0] = moved[0] - dot3(moved[1], scaled[0])
    moved[3] = moved[3] - dot3(moved[1], scaled[1])
    k1.gather_second()
    k0.gather_cores()
    k0.arrived()
    small[...] = plus_identity(whole(head0, 0))
    invert(small, scratch, (k1.gather_first, nothing, k1.gather_cores, nothing))
    k1.arrived()
    coeff = dot3(small[...], whole(head0, 1))
    result[...] = moved[3] - dot3(moved[0], coeff)
    store = pltpu.make_async_copy(result, out_hbm, out_sem)
    store.start()
    for copy in links.sent:
        copy.wait_send()
    store.wait()


COPIES = (1 + 15 + 1 + 15 + 1) + (1 + 12 + 1 + 12 + 1) + (1 + 12 + 1) + 2 * (17 + 14) + 1


def per_device(leaf_blocks, generators, right_side, tree_order):
    rows, rank = leaf_blocks.shape[0], generators.shape[2]
    dma = pltpu.SemaphoreType.DMA

    def buffer(*shape):
        return pltpu.VMEM(shape, F32)

    scratch = [
        buffer(rows, rows), buffer(3, rows, rank), buffer(rows, rank), pltpu.VMEM((1, rows), jnp.int32),
        buffer(4, rows, rank), buffer(4, rows, rank), buffer(rows, rank),
        buffer(9, 2, 2, 4, 4, 8, 128), buffer(9, 2, 4, 4, 8, 128), buffer(9, 2, 4, 4, 8, 128),
        buffer(3, 2, 9, 4, 8, 128), buffer(9, 2, 4, 8, 128), buffer(3, 2, 9, 8, 128),
        buffer(15, 1, 2, 8, 128),
        buffer(9, 2, 8, 128), buffer(9, 2, 8, 128), buffer(4, 2, 2, 4, 4, 8, 128),
        buffer(5, 2, 8, 128), buffer(5, 2, 8, 128), buffer(3, 2, 2, 4, 4, 8, 128),
        buffer(2, 2, 8, 128), buffer(2, 2, 8, 128), buffer(2, 2, 2, 4, 4, 8, 128),
        buffer(rank, rank), buffer(3, rank, rank),
        buffer(2, 8, 8, BASE), buffer(2, 8, BASE), buffer(BASE, rows), buffer(rows, BASE),
        dma((4,)), dma(()), dma((COPIES, 2)),
    ]
    hbm = pl.BlockSpec(memory_space=pltpu.MemorySpace.HBM)
    return pl.pallas_call(
        kernel,
        out_shape=jax.ShapeDtypeStruct(right_side.shape, F32),
        in_specs=[hbm] * 4,
        out_specs=hbm,
        scratch_shapes=scratch,
        compiler_params=pltpu.CompilerParams(
            collective_id=0, has_side_effects=True, vmem_limit_bytes=VMEM_LIMIT
        ),
        name="solve",
    )(leaf_blocks, generators, right_side, tree_order)


def solution(mesh):
    return jax.shard_map(
        per_device,
        mesh=mesh,
        in_specs=(
            P(("leaf", "node"), None),
            P(None, ("leaf", "node"), None),
            P(("leaf", "node"), None),
            P(("leaf", "node"), None),
        ),
        out_specs=P(("leaf", "node"), None),
        check_vma=False,
    )
```

```python
import functools

import jax
import jax.numpy as jnp
from jax import lax
from jax.experimental import pallas as pl
from jax.experimental.pallas import tpu as pltpu
from jax.sharding import PartitionSpec as P

F32 = jnp.float32
BF16 = jnp.bfloat16
MESH = pl.DeviceIdType.MESH
NN = (((1,), (0,)), ((), ()))
NT = (((1,), (1,)), ((), ()))
TN = (((0,), (0,)), ((), ()))
BASE = 128
VMEM_LIMIT = 64 * 2**20 - 3 * 2**18


def split(value):
    high = value.astype(BF16)
    return high, (value - high.astype(F32)).astype(BF16)


def dot3(left, right, dims=NN):
    left_high, left_low = split(left)
    right_high, right_low = split(right)
    one = functools.partial(lax.dot_general, dimension_numbers=dims, preferred_element_type=F32)
    return one(left_high, right_high) + (one(left_high, right_low) + one(left_low, right_high))


def dot6(left, right, dims=NN):
    return lax.dot_general(
        left, right, dims, precision=lax.Precision.HIGHEST, preferred_element_type=F32
    )


def permute(one_hot, value, dims):
    high = value.astype(BF16)
    rest = value - high.astype(F32)
    middle = rest.astype(BF16)
    low = (rest - middle.astype(F32)).astype(BF16)
    one = functools.partial(lax.dot_general, dimension_numbers=dims, preferred_element_type=F32)
    return one(one_hot, high) + (one(one_hot, middle) + one(one_hot, low))


def ldl_factor(p):
    p = [list(row) for row in p]
    n = len(p)
    lower = [[None] * n for _ in range(n)]
    pivots = []
    for k in range(n):
        r = 1.0 / p[k][k]
        pivots.append(r)
        raw = [p[i][k] for i in range(n)] if k == 0 else [p[i][k] if i > k else None for i in range(n)]
        for i in range(k + 1, n):
            for j in range(k + 1, i + 1):
                p[i][j] = p[i][j] - r * (raw[i] * raw[j])
        for i in range(k + 1, n):
            lower[i][k] = raw[i] * r
    return lower, pivots


def ldl_solve(lower, pivots, rows):
    n = len(rows)
    y = list(rows)
    for k in range(n):
        for i in range(k + 1, n):
            y[i] = y[i] - lower[i][k] * y[k]
    z = [y[i] * pivots[i] for i in range(n)]
    for k in range(n - 1, -1, -1):
        for i in range(k):
            z[i] = z[i] - lower[k][i] * z[k]
    return z


def nothing():
    pass


def base_inverse(a, columns_ref, rows_ref, halfway):
    n = a.shape[0]
    lane8 = lax.broadcasted_iota(jnp.int32, (8, n), 1)
    sub8 = lax.broadcasted_iota(jnp.int32, (8, n), 0)
    lane = lax.broadcasted_iota(jnp.int32, (n, n), 1)
    for kb in range(n // 8):
        if kb == n // 16:
            halfway()
        k = 8 * kb
        slot = kb % 2
        own = a[k : k + 8, :]
        for j in range(8):
            column = jnp.sum(jnp.where(lane8 == k + j, own, 0.0), axis=1, keepdims=True)
            columns_ref[slot, j] = jnp.broadcast_to(column, (8, n))
        inside = (lane8 >= k) & (lane8 < k + 8)
        rows_ref[slot] = jnp.where(inside, jnp.where(lane8 == sub8 + k, 1.0, 0.0), own)
        p = [
            [jnp.broadcast_to(columns_ref[slot, j, i : i + 1, :], (8, n)) for j in range(i + 1)]
            for i in range(8)
        ]
        rows = [jnp.broadcast_to(rows_ref[slot, i : i + 1, :], (8, n)) for i in range(8)]
        q = ldl_solve(*ldl_factor(p), rows)
        own = q[0]
        for j in range(1, 8):
            own = jnp.where(sub8 == j, q[j], own)
        rest = jnp.where((lane >= k) & (lane < k + 8), 0.0, a)
        terms = [
            jnp.sum(jnp.where(lane == k + j, a, 0.0), axis=1, keepdims=True)
            * jnp.broadcast_to(q[j][0:1, :], (n, n))
            for j in range(8)
        ]
        while len(terms) > 1:
            terms = [terms[i] + terms[i + 1] for i in range(0, len(terms), 2)]
        rest = rest - terms[0]
        parts = [rest[:k]] if k else []
        parts.append(own)
        if k + 8 < n:
            parts.append(rest[k + 8 :])
        a = jnp.concatenate(parts, axis=0)
    return a


def invert(a_ref, scratch, hooks=None):
    columns_ref, rows_ref, row_block, column_block = scratch
    n = a_ref.shape[0]
    eye = (
        lax.broadcasted_iota(jnp.int32, (BASE, BASE), 0)
        == lax.broadcasted_iota(jnp.int32, (BASE, BASE), 1)
    ).astype(F32)

    def step(own, halfway=nothing, inverted=nothing):
        pivot = base_inverse(a_ref[own, own], columns_ref, rows_ref, halfway)
        inverted()
        row_block[:, :n] = a_ref[own, :]
        row_block[:, own] = eye
        column_block[:n, :] = a_ref[:, own]
        a_ref[:, own] = jnp.zeros((n, BASE), F32)
        q = dot6(pivot, row_block[:, :n])
        a_ref[...] = a_ref[...] - dot6(column_block[:n, :], q)
        a_ref[own, :] = q

    if hooks is None:
        def body(kb, carry):
            step(pl.ds(pl.multiple_of(kb * BASE, BASE), BASE))
            return carry

        lax.fori_loop(0, n // BASE, body, 0)
        return
    for kb in range(n // BASE):
        step(pl.ds(kb * BASE, BASE), *hooks[3 * kb : 3 * kb + 2])
        hooks[3 * kb + 2]()


PAIRS = ((2, 2), (1, 2), (0, 2), (2, 3), (1, 1), (0, 1), (1, 3), (0, 0), (0, 3))


def place():
    leaf_index = lax.axis_index("leaf")
    return leaf_index // 8, (leaf_index // 2) % 4, leaf_index % 2, lax.axis_index("node")


def device(z, x, core, y):
    return ((z * 4 + x) * 2 + core, y)


class Links:
    def __init__(self, sems):
        self.sems = sems
        self.used = 0
        self.sent = []
        self.z, self.x, self.core, self.y = place()
        self.across = device(self.z, self.x, 1 - self.core, self.y)

    def along(self, axis, step):
        if axis == "x":
            index = lax.rem(self.x + step, 4)
            return index, device(self.z, index, self.core, self.y)
        index = lax.rem(self.y + step, 4)
        return index, device(self.z, self.x, self.core, index)

    def above(self, bit, step=0):
        return device(self.z ^ (1 << bit), self.x, self.core, lax.rem(self.y + step, 4))

    def partners(self):
        near = [self.along(axis, step)[1] for axis in "xy" for step in (1, 2, 3)]
        far = [self.above(bit, step) for bit in range(3) for step in range(4)]
        return near + [self.across] + far

    def send(self, source, target, to):
        copy = pltpu.make_async_remote_copy(
            src_ref=source, dst_ref=target, send_sem=self.sems.at[self.used, 0],
            recv_sem=self.sems.at[self.used, 1], device_id=to, device_id_type=MESH,
        )
        self.used += 1
        copy.start()
        self.sent.append(copy)
        return copy


class Group:
    def __init__(self, links, blocks, bit, part, from_z, head=None, plane=None):
        self.links, self.blocks, self.bit = links, blocks, bit
        self.part, self.from_z, self.head, self.plane = part, from_z, head, plane
        self.pending = []

    def arrived(self):
        for copy in self.pending:
            copy.wait_recv()
        self.pending = []

    def over_cores(self):
        gram, from_core = self.plane[:2]
        links, blocks = self.links, self.blocks
        source = gram.at[blocks, :, 1 - links.core]
        self.pending = [links.send(source, from_core.at[blocks], links.across)]

    def add_cores(self):
        gram, from_core, one = self.plane[:3]
        blocks = self.blocks
        self.arrived()
        one[blocks] = gram[blocks, :, self.links.core] + from_core[blocks]

    def over_first(self):
        one, from_one = self.plane[2:4]
        links, blocks = self.links, self.blocks
        self.add_cores()
        for step in (1, 2, 3):
            x, to_x = links.along("x", step)
            y, to_y = links.along("y", step)
            self.pending += [
                links.send(one.at[blocks, 0, x], from_one.at[step - 1, 0, blocks], to_x),
                links.send(one.at[blocks, 1, :, y], from_one.at[step - 1, 1, blocks], to_y),
            ]

    def over_second(self):
        one, from_one, two, from_two = self.plane[2:]
        links, blocks = self.links, self.blocks
        self.arrived()
        for half, own in enumerate((one[blocks, 0, links.x], one[blocks, 1, :, links.y])):
            two[blocks, half] = (own + from_one[0, half, blocks]) + (
                from_one[1, half, blocks] + from_one[2, half, blocks]
            )
        for step in (1, 2, 3):
            x, to_x = links.along("x", step)
            y, to_y = links.along("y", step)
            self.pending += [
                links.send(two.at[blocks, 0, y], from_two.at[step - 1, 0, blocks], to_y),
                links.send(two.at[blocks, 1, x], from_two.at[step - 1, 1, blocks], to_x),
            ]

    def add_plane(self):
        links, blocks = self.links, self.blocks
        self.arrived()
        if self.plane is not None:
            two, from_two = self.plane[4:]
            for half, own in enumerate((two[blocks, 0, links.y], two[blocks, 1, links.x])):
                self.part[blocks, half] = (own + from_two[0, half, blocks]) + (
                    from_two[1, half, blocks] + from_two[2, half, blocks]
                )

    def over_planes(self):
        links, blocks = self.links, self.blocks
        self.add_plane()
        self.pending = [
            links.send(self.part.at[blocks], self.from_z.at[blocks], links.above(self.bit))
        ]

    def summed(self):
        self.arrived()
        return self.part[self.blocks] + self.from_z[self.blocks]

    def spread(self, part, to):
        self.pending.append(self.links.send(part, part, to))

    def gather_pair(self, pair):
        links = self.links
        self.add_plane()
        self.pair = pair
        source = self.part.at[self.blocks]
        pair[0, :, :, links.y] = self.part[self.blocks]
        for step in range(4):
            if step:
                to = links.along("y", step)[1]
                self.pending.append(links.send(source, pair.at[0, :, :, links.y], to))
            to = links.above(self.bit, step)
            self.pending.append(links.send(source, pair.at[1, :, :, links.y], to))

    def gather_along(self):
        links = self.links
        self.arrived()
        self.head[self.blocks, :, links.core, links.x] = self.pair[0] + self.pair[1]
        for step in (1, 2, 3):
            part = self.head.at[self.blocks, :, links.core, links.x]
            self.spread(part, links.along("x", step)[1])

    def gather_second(self):
        links = self.links
        self.head[self.blocks, :, links.core, links.x, links.y] = self.summed()
        for step in (1, 2, 3):
            for half, axis in enumerate("yx"):
                part = self.head.at[self.blocks, half, links.core, links.x, links.y]
                self.spread(part, links.along(axis, step)[1])

    def gather_first(self):
        links = self.links
        self.arrived()
        for step in (1, 2, 3):
            self.spread(self.head.at[self.blocks, 0, links.core, links.x], links.along("x", step)[1])
            self.spread(
                self.head.at[self.blocks, 1, links.core, :, links.y], links.along("y", step)[1]
            )

    def gather_cores(self):
        links = self.links
        self.arrived()
        self.spread(self.head.at[self.blocks, :, links.core], links.across)


def one_hot_of(order_ref):
    n = order_ref.shape[1]
    target = lax.broadcasted_iota(jnp.int32, (n, n), 0)
    return jnp.where(target == order_ref[...], 1.0, 0.0).astype(BF16)


def whole(ref, index):
    return jnp.concatenate([ref[index, half].reshape(256, 128) for half in range(2)], axis=1)


def plus_identity(value):
    n = value.shape[0]
    eye = lax.broadcasted_iota(jnp.int32, (n, n), 0) == lax.broadcasted_iota(jnp.int32, (n, n), 1)
    return value + jnp.where(eye, 1.0, 0.0)


def kernel(
    leaf_hbm, gens_hbm, rhs_hbm, order_hbm, out_hbm,
    inverse, gens, rhs, order, x, moved, result,
    gram, from_core, one, from_one, two, from_two, pair2, pair1, pair0,
    part2, from2, head2, part1, from1, head1, part0, from0, head0,
    small, scaled, columns_ref, rows_ref, row_block, column_block,
    in_sems, out_sem, sems,
):
    scratch = (columns_ref, rows_ref, row_block, column_block)
    links = Links(sems)
    loads = [
        pltpu.make_async_copy(source, target, in_sems.at[i])
        for i, (source, target) in enumerate(
            ((leaf_hbm, inverse), (gens_hbm, gens), (rhs_hbm, rhs), (order_hbm, order))
        )
    ]
    for load in loads:
        load.start()
    barrier = pltpu.get_barrier_semaphore()
    partners = links.partners()
    for partner in partners:
        pl.semaphore_signal(barrier, inc=1, device_id=partner, device_id_type=MESH)

    loads[0].wait()
    invert(inverse, scratch)
    for load in loads[1:]:
        load.wait()

    def apply(value):
        return dot3(inverse[...], value)

    def product(index):
        a, b = PAIRS[index]
        value = dot3(gens[a], x[b], TN)
        for half in range(2):
            columns = value[:, half * 128 : half * 128 + 128]
            gram[index, half] = columns.reshape(gram.shape[2:])

    plane = (gram, from_core, one, from_one, two, from_two)
    g0, g1, g2 = (
        Group(links, blocks, 0, part2, from2, head2, plane)
        for blocks in (pl.ds(0, 1), pl.ds(1, 3), pl.ds(4, 5))
    )
    x[2] = apply(gens[2])
    product(0)
    pl.semaphore_wait(barrier, len(partners))
    g0.over_cores()
    product(1)
    g0.over_first()
    one_hot = one_hot_of(order)
    product(2)
    x[3] = apply(permute(one_hot, rhs[...], TN))
    g0.over_second()
    product(3)
    g1.over_cores()
    x[1] = apply(gens[1])
    g0.gather_pair(pair2)
    g1.over_first()
    product(4)
    product(5)
    product(6)
    x[0] = apply(gens[0])
    g0.gather_along()
    g1.over_second()
    product(7)
    product(8)
    g2.over_cores()
    moved[2] = permute(one_hot, x[2], NN)
    g0.gather_cores()
    g1.over_planes()
    g2.over_first()
    g0.arrived()
    small[...] = plus_identity(whole(head2, 0))

    def hook_two():
        g1.gather_second()
        g2.over_second()

    invert(
        small, scratch,
        (hook_two, nothing, g1.gather_first, g2.over_planes, g1.gather_cores, nothing),
    )

    def slices(target, index, head, a, scaled_b, old):
        rows = jnp.concatenate(
            [head[a, half, links.core, links.x, links.y] for half in range(2)], axis=1
        )
        for half in range(2):
            update = dot3(rows, scaled_b[:, half * 128 : half * 128 + 128])
            target[index, half] = old[index, half] - update

    h0, h1, h2 = (
        Group(links, blocks, 1, part1, from1, head1)
        for blocks in (pl.ds(0, 1), pl.ds(1, 2), pl.ds(3, 2))
    )
    g1.arrived()
    scaled[1] = dot3(small[...], whole(head2, 1), NT)
    rest2 = g2.summed()
    slices(part1, 0, head2, 1, scaled[1], rest2)
    h0.gather_pair(pair1)
    scaled[2] = dot3(small[...], whole(head2, 3))
    slices(part1, 1, head2, 2, scaled[1], rest2)
    slices(part1, 2, head2, 1, scaled[2], rest2)
    h1.over_planes()
    scaled[0] = dot3(small[...], whole(head2, 2), NT)
    slices(part1, 3, head2, 2, scaled[0], rest2)
    slices(part1, 4, head2, 2, scaled[2], rest2)
    h2.over_planes()
    h0.gather_along()
    moved[1] = permute(one_hot_of(order), x[1], NN) - dot3(moved[2], scaled[1])
    moved[0] = permute(one_hot_of(order), x[0], NN) - dot3(moved[2], scaled[0])
    h1.gather_second()
    h0.gather_cores()
    h0.arrived()
    small[...] = plus_identity(whole(head1, 0))
    invert(small, scratch, (h1.gather_first, nothing, nothing, h1.gather_cores, nothing, nothing))

    k0, k1 = (
        Group(links, blocks, 2, part0, from0, head0) for blocks in (pl.ds(0, 1), pl.ds(1, 1))
    )
    h1.arrived()
    scaled[0] = dot3(small[...], whole(head1, 1), NT)
    rest1 = h2.summed()
    slices(part0, 0, head1, 1, scaled[0], rest1)
    k0.gather_pair(pair0)
    scaled[1] = dot3(small[...], whole(head1, 2))
    slices(part0, 1, head1, 1, scaled[1], rest1)
    k1.over_planes()
    moved[3] = permute(one_hot_of(order), x[3], NN) - dot3(moved[2], scaled[2])
    k0.gather_along()
    moved[0] = moved[0] - dot3(moved[1], scaled[0])
    moved[3] = moved[3] - dot3(moved[1], scaled[1])
    k1.gather_second()
    k0.gather_cores()
    k0.arrived()
    small[...] = plus_identity(whole(head0, 0))
    invert(small, scratch, (k1.gather_first, nothing, nothing, k1.gather_cores, nothing, nothing))
    k1.arrived()
    coeff = dot3(small[...], whole(head0, 1))
    result[...] = moved[3] - dot3(moved[0], coeff)
    store = pltpu.make_async_copy(result, out_hbm, out_sem)
    store.start()
    for copy in links.sent:
        copy.wait_send()
    store.wait()


COPIES = (1 + 12 + 7 + 3 + 1) + (1 + 12 + 1 + 12 + 1) + (1 + 12 + 1) + 2 * (11 + 14) + 1


def per_device(leaf_blocks, generators, right_side, tree_order):
    rows, rank = leaf_blocks.shape[0], generators.shape[2]
    dma = pltpu.SemaphoreType.DMA

    def buffer(*shape):
        return pltpu.VMEM(shape, F32)

    scratch = [
        buffer(rows, rows), buffer(3, rows, rank), buffer(rows, rank), pltpu.VMEM((1, rows), jnp.int32),
        buffer(4, rows, rank), buffer(4, rows, rank), buffer(rows, rank),
        buffer(9, 2, 2, 4, 4, 8, 128), buffer(9, 2, 4, 4, 8, 128), buffer(9, 2, 4, 4, 8, 128),
        buffer(3, 2, 9, 4, 8, 128), buffer(9, 2, 4, 8, 128), buffer(3, 2, 9, 8, 128),
        buffer(2, 1, 2, 4, 8, 128), buffer(2, 1, 2, 4, 8, 128), buffer(2, 1, 2, 4, 8, 128),
        buffer(9, 2, 8, 128), buffer(9, 2, 8, 128), buffer(4, 2, 2, 4, 4, 8, 128),
        buffer(5, 2, 8, 128), buffer(5, 2, 8, 128), buffer(3, 2, 2, 4, 4, 8, 128),
        buffer(2, 2, 8, 128), buffer(2, 2, 8, 128), buffer(2, 2, 2, 4, 4, 8, 128),
        buffer(rank, rank), buffer(3, rank, rank),
        buffer(2, 8, 8, BASE), buffer(2, 8, BASE), buffer(BASE, rows), buffer(rows, BASE),
        dma((4,)), dma(()), dma((COPIES, 2)),
    ]
    hbm = pl.BlockSpec(memory_space=pltpu.MemorySpace.HBM)
    return pl.pallas_call(
        kernel,
        out_shape=jax.ShapeDtypeStruct(right_side.shape, F32),
        in_specs=[hbm] * 4,
        out_specs=hbm,
        scratch_shapes=scratch,
        compiler_params=pltpu.CompilerParams(
            collective_id=0, has_side_effects=True, vmem_limit_bytes=VMEM_LIMIT
        ),
        name="solve",
    )(leaf_blocks, generators, right_side, tree_order)


def solution(mesh):
    return jax.shard_map(
        per_device,
        mesh=mesh,
        in_specs=(
            P(("leaf", "node"), None),
            P(None, ("leaf", "node"), None),
            P(("leaf", "node"), None),
            P(("leaf", "node"), None),
        ),
        out_specs=P(("leaf", "node"), None),
        check_vma=False,
    )
```

```python
import functools

import jax
import jax.numpy as jnp
from jax import lax
from jax.experimental import pallas as pl
from jax.experimental.pallas import tpu as pltpu
from jax.sharding import PartitionSpec as P

F32 = jnp.float32
BF16 = jnp.bfloat16
MESH = pl.DeviceIdType.MESH
NN = (((1,), (0,)), ((), ()))
NT = (((1,), (1,)), ((), ()))
TN = (((0,), (0,)), ((), ()))
BASE = 128
VMEM_LIMIT = 64 * 2**20 - 3 * 2**18


def split(value):
    high = value.astype(BF16)
    return high, (value - high.astype(F32)).astype(BF16)


def dot3(left, right, dims=NN):
    left_high, left_low = split(left)
    right_high, right_low = split(right)
    one = functools.partial(lax.dot_general, dimension_numbers=dims, preferred_element_type=F32)
    return one(left_high, right_high) + (one(left_high, right_low) + one(left_low, right_high))


def dot6(left, right, dims=NN):
    return lax.dot_general(
        left, right, dims, precision=lax.Precision.HIGHEST, preferred_element_type=F32
    )


def permute(one_hot, value, dims):
    high = value.astype(BF16)
    rest = value - high.astype(F32)
    middle = rest.astype(BF16)
    low = (rest - middle.astype(F32)).astype(BF16)
    one = functools.partial(lax.dot_general, dimension_numbers=dims, preferred_element_type=F32)
    return one(one_hot, high) + (one(one_hot, middle) + one(one_hot, low))


def ldl_factor(p):
    p = [list(row) for row in p]
    n = len(p)
    lower = [[None] * n for _ in range(n)]
    pivots = []
    for k in range(n):
        r = 1.0 / p[k][k]
        pivots.append(r)
        raw = [p[i][k] for i in range(n)] if k == 0 else [p[i][k] if i > k else None for i in range(n)]
        for i in range(k + 1, n):
            for j in range(k + 1, i + 1):
                p[i][j] = p[i][j] - r * (raw[i] * raw[j])
        for i in range(k + 1, n):
            lower[i][k] = raw[i] * r
    return lower, pivots


def ldl_solve(lower, pivots, rows):
    n = len(rows)
    y = list(rows)
    for k in range(n):
        for i in range(k + 1, n):
            y[i] = y[i] - lower[i][k] * y[k]
    z = [y[i] * pivots[i] for i in range(n)]
    for k in range(n - 1, -1, -1):
        for i in range(k):
            z[i] = z[i] - lower[k][i] * z[k]
    return z


def nothing():
    pass


def base_inverse(a, columns_ref, rows_ref, halfway):
    n = a.shape[0]
    lane8 = lax.broadcasted_iota(jnp.int32, (8, n), 1)
    sub8 = lax.broadcasted_iota(jnp.int32, (8, n), 0)
    lane = lax.broadcasted_iota(jnp.int32, (n, n), 1)
    for kb in range(n // 8):
        if kb == n // 16:
            halfway()
        k = 8 * kb
        slot = kb % 2
        own = a[k : k + 8, :]
        for j in range(8):
            column = jnp.sum(jnp.where(lane8 == k + j, own, 0.0), axis=1, keepdims=True)
            columns_ref[slot, j] = jnp.broadcast_to(column, (8, n))
        inside = (lane8 >= k) & (lane8 < k + 8)
        rows_ref[slot] = jnp.where(inside, jnp.where(lane8 == sub8 + k, 1.0, 0.0), own)
        p = [
            [jnp.broadcast_to(columns_ref[slot, j, i : i + 1, :], (8, n)) for j in range(i + 1)]
            for i in range(8)
        ]
        rows = [jnp.broadcast_to(rows_ref[slot, i : i + 1, :], (8, n)) for i in range(8)]
        q = ldl_solve(*ldl_factor(p), rows)
        own = q[0]
        for j in range(1, 8):
            own = jnp.where(sub8 == j, q[j], own)
        rest = jnp.where((lane >= k) & (lane < k + 8), 0.0, a)
        terms = [
            jnp.sum(jnp.where(lane == k + j, a, 0.0), axis=1, keepdims=True)
            * jnp.broadcast_to(q[j][0:1, :], (n, n))
            for j in range(8)
        ]
        for term in terms:
            rest = rest - term
        parts = [rest[:k]] if k else []
        parts.append(own)
        if k + 8 < n:
            parts.append(rest[k + 8 :])
        a = jnp.concatenate(parts, axis=0)
    return a


def invert(a_ref, scratch, hooks=None):
    columns_ref, rows_ref, row_block, column_block = scratch
    n = a_ref.shape[0]
    eye = (
        lax.broadcasted_iota(jnp.int32, (BASE, BASE), 0)
        == lax.broadcasted_iota(jnp.int32, (BASE, BASE), 1)
    ).astype(F32)

    def step(own, halfway=nothing, inverted=nothing):
        pivot = base_inverse(a_ref[own, own], columns_ref, rows_ref, halfway)
        inverted()
        row_block[:, :n] = a_ref[own, :]
        row_block[:, own] = eye
        column_block[:n, :] = a_ref[:, own]
        a_ref[:, own] = jnp.zeros((n, BASE), F32)
        q = dot6(pivot, row_block[:, :n])
        a_ref[...] = a_ref[...] - dot3(column_block[:n, :], q)
        a_ref[own, :] = q

    if hooks is None:
        def body(kb, carry):
            step(pl.ds(pl.multiple_of(kb * BASE, BASE), BASE))
            return carry

        lax.fori_loop(0, n // BASE, body, 0)
        return
    for kb in range(n // BASE):
        step(pl.ds(kb * BASE, BASE), *hooks[3 * kb : 3 * kb + 2])
        hooks[3 * kb + 2]()


PAIRS = ((2, 2), (1, 2), (0, 2), (2, 3), (1, 1), (0, 1), (1, 3), (0, 0), (0, 3))


def place():
    leaf_index = lax.axis_index("leaf")
    return leaf_index // 8, (leaf_index // 2) % 4, leaf_index % 2, lax.axis_index("node")


def device(z, x, core, y):
    return ((z * 4 + x) * 2 + core, y)


class Links:
    def __init__(self, sems):
        self.sems = sems
        self.used = 0
        self.sent = []
        self.z, self.x, self.core, self.y = place()
        self.across = device(self.z, self.x, 1 - self.core, self.y)

    def along(self, axis, step):
        if axis == "x":
            index = lax.rem(self.x + step, 4)
            return index, device(self.z, index, self.core, self.y)
        index = lax.rem(self.y + step, 4)
        return index, device(self.z, self.x, self.core, index)

    def above(self, bit, step=0):
        return device(self.z ^ (1 << bit), self.x, self.core, lax.rem(self.y + step, 4))

    def partners(self):
        near = [self.along(axis, step)[1] for axis in "xy" for step in (1, 2, 3)]
        far = [self.above(bit, step) for bit in range(3) for step in range(4)]
        return near + [self.across] + far

    def send(self, source, target, to):
        copy = pltpu.make_async_remote_copy(
            src_ref=source, dst_ref=target, send_sem=self.sems.at[self.used, 0],
            recv_sem=self.sems.at[self.used, 1], device_id=to, device_id_type=MESH,
        )
        self.used += 1
        copy.start()
        self.sent.append(copy)
        return copy


class Group:
    def __init__(self, links, blocks, bit, part, from_z, head=None, plane=None):
        self.links, self.blocks, self.bit = links, blocks, bit
        self.part, self.from_z, self.head, self.plane = part, from_z, head, plane
        self.pending = []

    def arrived(self):
        for copy in self.pending:
            copy.wait_recv()
        self.pending = []

    def over_cores(self):
        gram, from_core = self.plane[:2]
        links, blocks = self.links, self.blocks
        source = gram.at[blocks, :, 1 - links.core]
        self.pending = [links.send(source, from_core.at[blocks], links.across)]

    def add_cores(self):
        gram, from_core, one = self.plane[:3]
        blocks = self.blocks
        self.arrived()
        one[blocks] = gram[blocks, :, self.links.core] + from_core[blocks]

    def over_first(self):
        one, from_one = self.plane[2:4]
        links, blocks = self.links, self.blocks
        self.add_cores()
        for step in (2, 1, 3):
            x, to_x = links.along("x", step)
            y, to_y = links.along("y", step)
            self.pending += [
                links.send(one.at[blocks, 0, x], from_one.at[step - 1, 0, blocks], to_x),
                links.send(one.at[blocks, 1, :, y], from_one.at[step - 1, 1, blocks], to_y),
            ]

    def over_second(self):
        one, from_one, two, from_two = self.plane[2:]
        links, blocks = self.links, self.blocks
        self.arrived()
        for half, own in enumerate((one[blocks, 0, links.x], one[blocks, 1, :, links.y])):
            two[blocks, half] = (own + from_one[0, half, blocks]) + (
                from_one[1, half, blocks] + from_one[2, half, blocks]
            )
        for step in (2, 1, 3):
            x, to_x = links.along("x", step)
            y, to_y = links.along("y", step)
            self.pending += [
                links.send(two.at[blocks, 0, y], from_two.at[step - 1, 0, blocks], to_y),
                links.send(two.at[blocks, 1, x], from_two.at[step - 1, 1, blocks], to_x),
            ]

    def add_plane(self):
        links, blocks = self.links, self.blocks
        self.arrived()
        if self.plane is not None:
            two, from_two = self.plane[4:]
            for half, own in enumerate((two[blocks, 0, links.y], two[blocks, 1, links.x])):
                self.part[blocks, half] = (own + from_two[0, half, blocks]) + (
                    from_two[1, half, blocks] + from_two[2, half, blocks]
                )

    def over_planes(self):
        links, blocks = self.links, self.blocks
        self.add_plane()
        self.pending = [
            links.send(self.part.at[blocks], self.from_z.at[blocks], links.above(self.bit))
        ]

    def summed(self):
        self.arrived()
        return self.part[self.blocks] + self.from_z[self.blocks]

    def spread(self, part, to):
        self.pending.append(self.links.send(part, part, to))

    def gather_pair(self, pair):
        links = self.links
        self.add_plane()
        self.pair = pair
        source = self.part.at[self.blocks]
        pair[0, :, :, links.y] = self.part[self.blocks]
        for step in (2, 1, 3, 0):
            to = links.above(self.bit, step)
            self.pending.append(links.send(source, pair.at[1, :, :, links.y], to))
        for step in (2, 1, 3):
            to = links.along("y", step)[1]
            self.pending.append(links.send(source, pair.at[0, :, :, links.y], to))

    def gather_along(self):
        links = self.links
        self.arrived()
        self.head[self.blocks, :, links.core, links.x] = self.pair[0] + self.pair[1]
        for step in (2, 1, 3):
            part = self.head.at[self.blocks, :, links.core, links.x]
            self.spread(part, links.along("x", step)[1])

    def gather_second(self):
        links = self.links
        self.head[self.blocks, :, links.core, links.x, links.y] = self.summed()
        for step in (2, 1, 3):
            for half, axis in enumerate("yx"):
                part = self.head.at[self.blocks, half, links.core, links.x, links.y]
                self.spread(part, links.along(axis, step)[1])

    def gather_first(self):
        links = self.links
        self.arrived()
        for step in (2, 1, 3):
            self.spread(self.head.at[self.blocks, 0, links.core, links.x], links.along("x", step)[1])
            self.spread(
                self.head.at[self.blocks, 1, links.core, :, links.y], links.along("y", step)[1]
            )

    def gather_cores(self):
        links = self.links
        self.arrived()
        self.spread(self.head.at[self.blocks, :, links.core], links.across)


def one_hot_of(order_ref):
    n = order_ref.shape[1]
    target = lax.broadcasted_iota(jnp.int32, (n, n), 0)
    return jnp.where(target == order_ref[...], 1.0, 0.0).astype(BF16)


def whole(ref, index):
    return jnp.concatenate([ref[index, half].reshape(256, 128) for half in range(2)], axis=1)


def plus_identity(value):
    n = value.shape[0]
    eye = lax.broadcasted_iota(jnp.int32, (n, n), 0) == lax.broadcasted_iota(jnp.int32, (n, n), 1)
    return value + jnp.where(eye, 1.0, 0.0)


def kernel(
    leaf_hbm, gens_hbm, rhs_hbm, order_hbm, out_hbm,
    inverse, gens, rhs, order, x, moved, result,
    gram, from_core, one, from_one, two, from_two, pair2, pair1, pair0,
    part2, from2, head2, part1, from1, head1, part0, from0, head0,
    small, scaled, columns_ref, rows_ref, row_block, column_block,
    in_sems, out_sems, sems,
):
    scratch = (columns_ref, rows_ref, row_block, column_block)
    links = Links(sems)
    loads = [
        pltpu.make_async_copy(source, target, in_sems.at[i])
        for i, (source, target) in enumerate(
            ((leaf_hbm, inverse), (gens_hbm, gens), (rhs_hbm, rhs), (order_hbm, order))
        )
    ]
    for load in loads:
        load.start()
    barrier = pltpu.get_barrier_semaphore()
    partners = links.partners()
    for partner in partners:
        pl.semaphore_signal(barrier, inc=1, device_id=partner, device_id_type=MESH)

    loads[0].wait()
    invert(inverse, scratch)
    for load in loads[1:]:
        load.wait()

    def apply(value):
        return dot3(inverse[...], value)

    def product(index):
        a, b = PAIRS[index]
        value = dot3(gens[a], x[b], TN)
        for half in range(2):
            columns = value[:, half * 128 : half * 128 + 128]
            gram[index, half] = columns.reshape(gram.shape[2:])

    plane = (gram, from_core, one, from_one, two, from_two)
    g0, g1, g2 = (
        Group(links, blocks, 0, part2, from2, head2, plane)
        for blocks in (pl.ds(0, 1), pl.ds(1, 3), pl.ds(4, 5))
    )
    x[2] = apply(gens[2])
    product(0)
    pl.semaphore_wait(barrier, len(partners))
    g0.over_cores()
    product(1)
    g0.over_first()
    one_hot = one_hot_of(order)
    product(2)
    x[3] = apply(permute(one_hot, rhs[...], TN))
    g0.over_second()
    product(3)
    g1.over_cores()
    x[1] = apply(gens[1])
    g0.gather_pair(pair2)
    g1.over_first()
    product(4)
    product(5)
    product(6)
    x[0] = apply(gens[0])
    g0.gather_along()
    g1.over_second()
    product(7)
    product(8)
    g2.over_cores()
    moved[2] = permute(one_hot, x[2], NN)
    g0.gather_cores()
    g1.over_planes()
    g2.over_first()
    g0.arrived()
    small[...] = plus_identity(whole(head2, 0))

    def hook_two():
        g1.gather_second()
        g2.over_second()

    invert(
        small, scratch,
        (hook_two, nothing, g1.gather_first, g2.over_planes, g1.gather_cores, nothing),
    )

    def slices(target, index, head, a, scaled_b, old):
        rows = jnp.concatenate(
            [head[a, half, links.core, links.x, links.y] for half in range(2)], axis=1
        )
        for half in range(2):
            update = dot3(rows, scaled_b[:, half * 128 : half * 128 + 128])
            target[index, half] = old[index, half] - update

    h0, h1, h2 = (
        Group(links, blocks, 1, part1, from1, head1)
        for blocks in (pl.ds(0, 1), pl.ds(1, 2), pl.ds(3, 2))
    )
    g1.arrived()
    scaled[1] = dot3(small[...], whole(head2, 1), NT)
    rest2 = g2.summed()
    slices(part1, 0, head2, 1, scaled[1], rest2)
    h0.gather_pair(pair1)
    scaled[2] = dot3(small[...], whole(head2, 3))
    slices(part1, 1, head2, 2, scaled[1], rest2)
    slices(part1, 2, head2, 1, scaled[2], rest2)
    h1.over_planes()
    scaled[0] = dot3(small[...], whole(head2, 2), NT)
    slices(part1, 3, head2, 2, scaled[0], rest2)
    slices(part1, 4, head2, 2, scaled[2], rest2)
    h2.over_planes()
    h0.gather_along()
    moved[1] = permute(one_hot_of(order), x[1], NN) - dot3(moved[2], scaled[1])
    moved[0] = permute(one_hot_of(order), x[0], NN) - dot3(moved[2], scaled[0])
    h1.gather_second()
    h0.gather_cores()
    h0.arrived()
    small[...] = plus_identity(whole(head1, 0))
    invert(small, scratch, (h1.gather_first, nothing, nothing, h1.gather_cores, nothing, nothing))

    k0, k1 = (
        Group(links, blocks, 2, part0, from0, head0) for blocks in (pl.ds(0, 1), pl.ds(1, 1))
    )
    h1.arrived()
    scaled[0] = dot3(small[...], whole(head1, 1), NT)
    rest1 = h2.summed()
    slices(part0, 0, head1, 1, scaled[0], rest1)
    k0.gather_pair(pair0)
    scaled[1] = dot3(small[...], whole(head1, 2))
    slices(part0, 1, head1, 1, scaled[1], rest1)
    k1.over_planes()
    moved[3] = permute(one_hot_of(order), x[3], NN) - dot3(moved[2], scaled[2])
    k0.gather_along()
    moved[0] = moved[0] - dot3(moved[1], scaled[0])
    moved[3] = moved[3] - dot3(moved[1], scaled[1])
    k1.gather_second()
    k0.gather_cores()
    k0.arrived()
    small[...] = plus_identity(whole(head0, 0))
    invert(small, scratch, (k1.gather_first, nothing, nothing, k1.gather_cores, nothing, nothing))
    k1.arrived()
    coeff = dot3(small[...], whole(head0, 1))
    stores = []
    for index in range(2):
        rows = pl.ds(index * 256, 256)
        result[rows] = moved[3, rows] - dot3(moved[0, rows], coeff)
        store = pltpu.make_async_copy(result.at[rows], out_hbm.at[rows], out_sems.at[index])
        store.start()
        stores.append(store)
    for copy in links.sent:
        copy.wait_send()
    for store in stores:
        store.wait()


COPIES = (1 + 12 + 7 + 3 + 1) + (1 + 12 + 1 + 12 + 1) + (1 + 12 + 1) + 2 * (11 + 14) + 1


def per_device(leaf_blocks, generators, right_side, tree_order):
    rows, rank = leaf_blocks.shape[0], generators.shape[2]
    dma = pltpu.SemaphoreType.DMA

    def buffer(*shape):
        return pltpu.VMEM(shape, F32)

    scratch = [
        buffer(rows, rows), buffer(3, rows, rank), buffer(rows, rank), pltpu.VMEM((1, rows), jnp.int32),
        buffer(4, rows, rank), buffer(4, rows, rank), buffer(rows, rank),
        buffer(9, 2, 2, 4, 4, 8, 128), buffer(9, 2, 4, 4, 8, 128), buffer(9, 2, 4, 4, 8, 128),
        buffer(3, 2, 9, 4, 8, 128), buffer(9, 2, 4, 8, 128), buffer(3, 2, 9, 8, 128),
        buffer(2, 1, 2, 4, 8, 128), buffer(2, 1, 2, 4, 8, 128), buffer(2, 1, 2, 4, 8, 128),
        buffer(9, 2, 8, 128), buffer(9, 2, 8, 128), buffer(4, 2, 2, 4, 4, 8, 128),
        buffer(5, 2, 8, 128), buffer(5, 2, 8, 128), buffer(3, 2, 2, 4, 4, 8, 128),
        buffer(2, 2, 8, 128), buffer(2, 2, 8, 128), buffer(2, 2, 2, 4, 4, 8, 128),
        buffer(rank, rank), buffer(3, rank, rank),
        buffer(2, 8, 8, BASE), buffer(2, 8, BASE), buffer(BASE, rows), buffer(rows, BASE),
        dma((4,)), dma((2,)), dma((COPIES, 2)),
    ]
    hbm = pl.BlockSpec(memory_space=pltpu.MemorySpace.HBM)
    return pl.pallas_call(
        kernel,
        out_shape=jax.ShapeDtypeStruct(right_side.shape, F32),
        in_specs=[hbm] * 4,
        out_specs=hbm,
        scratch_shapes=scratch,
        compiler_params=pltpu.CompilerParams(
            collective_id=0, has_side_effects=True, vmem_limit_bytes=VMEM_LIMIT
        ),
        name="solve",
    )(leaf_blocks, generators, right_side, tree_order)


def solution(mesh):
    return jax.shard_map(
        per_device,
        mesh=mesh,
        in_specs=(
            P(("leaf", "node"), None),
            P(None, ("leaf", "node"), None),
            P(("leaf", "node"), None),
            P(("leaf", "node"), None),
        ),
        out_specs=P(("leaf", "node"), None),
        check_vma=False,
    )
```
